32 devices in a mesh: lat: 4 (over y, core), lon: 8 (over z, x).
Axes of the slice: x: 2, y: 2, z: 4, core: 2. Of those that a mesh axis runs over, the one named last changes fastest.
Arguments:
- background_expectation: float32 [3, 32, 1024], P(None, 'lat', 'lon'), may hold values from -6 to 6
- factor: float32 [32, 3, 32, 1024], P(None, None, 'lat', 'lon'), may hold values from -6 to 6
- average_thickness: float32 [32, 1024], P('lat', 'lon'), may hold values from 1 to 2
- obs_cells: int32 [8192], P(('lat', 'lon')), may hold values from 0 to 1023
- obs_count: int32 [32], P(('lat', 'lon')), may hold values from 64 to 256, as said below
- obs_values: float32 [8192], P(('lat', 'lon')), may hold values from -384 to 384
- obs_error: float32 [8192], P(('lat', 'lon')), may hold values from 20 to 200
Outputs:
- updated_expectation: float32 [3, 32, 1024], P(None, 'lat', 'lon')
- analysis_factor: float32 [32, 3, 32, 1024], P(None, None, 'lat', 'lon')
The draws below stay inside these ranges and needn't reach their ends.
Inputs may be any that keep to these rules, and one draw needn't show every extreme that they name: `obs_cells`: each entry is a cell of the block of the device that holds the slot, row-major over its 8 x 128 cells. Device d uses its first obs_count[d] slots; some device uses all 256.
All inputs are finite; a program needn't handle non-finite values.
Results may differ from the reference program's by a relative error of at most 0.00027.
Values sent between devices are 32-bit elements; how exact they have to be, the bound alone decides.
A program may use at most 64 MiB of HBM per device.

```python
import math
import jax
import jax.numpy as jnp
from jax import lax

SPREAD_RANK = 32
STEPS = 4
LAT_DEV = 8
LON_DEV = 128
OBS_DEV = 256
MERIDIAN_CELLS = 32
PARALLEL_CELLS = 1024
NOBS = 8192
N_LON = 8
DEVICES = 32


def draw_obs_count(key, part):
    first_key, second_key = jax.random.split(jax.random.fold_in(key, 17))
    counts = jax.random.randint(first_key, (DEVICES,), OBS_DEV // 4, OBS_DEV + 1)
    chosen = jax.random.randint(second_key, (), 0, DEVICES)
    return jnp.where(jnp.arange(DEVICES) == chosen, OBS_DEV, counts).astype(jnp.int32)


def set_ends(drawn, rng, low, largest):
    dims = drawn.shape
    spot = [jax.random.randint(jax.random.fold_in(rng, axis), (), 0, dims[axis]) for axis in range(len(dims))]
    drawn = drawn.at[tuple(spot)].set(low)
    longest = dims.index(max(dims))
    spot[longest] = (spot[longest] + 1) % dims[longest]
    return drawn.at[tuple(spot)].set(largest)


def shard_levels(own_key, extent, shards, low, top_value):
    loudness, own = 1.0, jax.random.fold_in(own_key, 6)
    for axis_at, blocks in shards:
        heights = jnp.exp(jax.random.uniform(jax.random.fold_in(own, axis_at), (blocks,), jnp.float32, low / len(shards), top_value / len(shards)))
        loudness = loudness * jnp.repeat(heights, extent[axis_at] // blocks).reshape([-1 if axis == axis_at else 1 for axis in range(len(extent))])
    return loudness


def gaussian(rng, dims, deviation, reach, pieces=(), held_as=jnp.bfloat16):
    entries = jax.random.normal(rng, dims, jnp.float32) * deviation
    if len(pieces) > 0:
        entries = shard_levels(rng, dims, pieces, -0.22, 0.18) * entries
    return jnp.clip(entries, min=-reach, max=reach).astype(held_as)


def setup_inputs(seed: int = 0) -> dict:
    streams_of = jax.random.split(jax.random.key(seed), 8)
    return {
        "background_expectation": gaussian(streams_of[0], (3, MERIDIAN_CELLS, PARALLEL_CELLS), 1.0, 6.0, ((1, 4), (2, 8)), jnp.float32),
        "factor": gaussian(streams_of[1], (SPREAD_RANK, 3, MERIDIAN_CELLS, PARALLEL_CELLS), 1.0, 6.0, ((2, 4), (3, 8)), jnp.float32),
        "average_thickness": jnp.clip(jnp.exp(math.log(2.0) - 0.6931472 * jax.random.uniform(streams_of[2], (MERIDIAN_CELLS, PARALLEL_CELLS), jnp.float32) ** shard_levels(streams_of[2], (MERIDIAN_CELLS, PARALLEL_CELLS), ((0, 4), (1, 8)), -0.2, 0.2)), 1.0, 2.0),
        "obs_cells": set_ends(jax.random.randint(streams_of[3], (NOBS,), 0, LAT_DEV * LON_DEV), jax.random.fold_in(streams_of[3], 1), 0, (LAT_DEV * LON_DEV) - 1).astype(jnp.int32),
        "obs_count": draw_obs_count(jax.random.fold_in(streams_of[7], 71), 0),
        "obs_values": gaussian(streams_of[5], (NOBS,), 60.0, 384.0, ((0, 32),), jnp.float32),
        "obs_error": jnp.clip(jnp.exp(math.log(200.0) - 2.3025851 * jax.random.uniform(streams_of[6], (NOBS,), jnp.float32) ** shard_levels(streams_of[6], (NOBS,), ((0, 32),), -0.2, 0.2)), 20.0, 200.0),
    }


TIME_STEP = 0.9
ROTATION = 0.25

def lon_diff(field):
    return 0.5 * (jnp.roll(field, -1, 1) - jnp.roll(field, 1, 1))

def lat_diff(field):
    padded = jnp.pad(field, ((1, 1), (0, 0)))
    return 0.5 * (padded[2:] - padded[:-2])

def advanced_spread_vector(spread_vector, average_thickness):
    height, east_wind, north_wind = (spread_vector[0], spread_vector[1], spread_vector[2])
    for repeat in range(STEPS):
        divergence = lon_diff(east_wind) + lat_diff(north_wind)
        height = height - TIME_STEP * average_thickness * divergence
        new_east = east_wind - TIME_STEP * lon_diff(height) + ROTATION * north_wind
        north_wind = north_wind - TIME_STEP * lat_diff(height) - ROTATION * east_wind
        east_wind = new_east
    return jnp.stack([height, east_wind, north_wind], 0)

def reference(background_expectation, factor, average_thickness, obs_cells, obs_count, obs_values, obs_error):
    joined_components = jnp.concatenate([background_expectation[None], factor], 0)
    propagated_spread = lax.map(lambda spread_vector: advanced_spread_vector(spread_vector, average_thickness), joined_components)
    position = jnp.arange(NOBS, dtype=jnp.int32)
    device = position // OBS_DEV
    band = device // N_LON
    cycle = device % N_LON
    row_index = band * LAT_DEV + obs_cells // LON_DEV
    col_index = cycle * LON_DEV + obs_cells % LON_DEV
    global_cell = (row_index * PARALLEL_CELLS + col_index).astype(jnp.int32)
    live = (position % OBS_DEV < obs_count[device]).astype(jnp.float32)
    weight = live / obs_error
    surface_elevation = propagated_spread[:, 0].reshape(SPREAD_RANK + 1, MERIDIAN_CELLS * PARALLEL_CELLS)
    picked = jnp.take(surface_elevation, global_cell, axis=1)
    scaled = picked[1:] * weight
    innovation = (obs_values - picked[0]) * weight
    gram = jnp.dot(scaled, scaled.T, precision=lax.Precision.HIGHEST)
    drive = jnp.dot(scaled, innovation, precision=lax.Precision.HIGHEST)
    identity = jnp.eye(SPREAD_RANK, dtype=jnp.float32)
    system = identity + gram
    lower = jnp.linalg.cholesky(system)
    inverse = lax.linalg.triangular_solve(lower, identity, left_side=True, lower=True, transpose_a=True)
    middle = lax.linalg.triangular_solve(lower, drive[:, None], left_side=True, lower=True)
    difference_coefficients = lax.linalg.triangular_solve(lower, middle, left_side=True, lower=True, transpose_a=True)[:, 0]
    sample_realisations = propagated_spread[1:].reshape(SPREAD_RANK, -1)
    analysis_factor = jnp.dot(inverse.T, sample_realisations, precision=lax.Precision.HIGHEST).reshape(factor.shape)
    updated_expectation = propagated_spread[0] + jnp.dot(difference_coefficients, sample_realisations, precision=lax.Precision.HIGHEST).reshape(background_expectation.shape)
    return (updated_expectation, analysis_factor)
```

```python
import functools

import jax
import jax.numpy as jnp
from jax import lax
from jax.experimental import pallas as pl
from jax.experimental.pallas import tpu as pltpu
from jax.sharding import PartitionSpec as P

STEPS = 4
TIME_STEP = 0.9
ROTATION = 0.25
MESH = pl.DeviceIdType.MESH
T = 8
NT = (((1,), (1,)), ((), ()))
HIGHEST = lax.Precision.HIGHEST


def roll(x, shift, axis=1):
    shift = shift % x.shape[axis]
    return x if shift == 0 else pltpu.roll(x, shift, axis)


def evolve(h, e, n, coef, up_gain, down_gain, band):
    half = 0.5 * TIME_STEP
    for step in range(STEPS):
        w = 2 * (STEPS - step)
        last = coef.shape[0] - T * (band - w + 1)
        mid = e[T:-T]
        div = (roll(mid, -1) - roll(mid, 1)) + (n[2 * T :] - n[: -2 * T])
        hn = h[T:-T] - coef[T * (band - w + 1) : last] * div
        inner = hn[T:-T]
        shape = (T * (w - 2), h.shape[1])
        parts = [jnp.full((T * band, h.shape[1]), half, jnp.float32)]
        if w > 2:
            parts = [jnp.full(shape, up_gain)] + parts + [jnp.full(shape, down_gain)]
        gain = jnp.concatenate(parts, 0) if w > 2 else parts[0]
        e0, n0 = e[2 * T : -2 * T], n[2 * T : -2 * T]
        e = e0 - half * (roll(inner, -1) - roll(inner, 1)) + ROTATION * n0
        n = n0 - gain * (hn[2 * T :] - hn[: -2 * T]) - ROTATION * e0
        h = inner
    return h, e, n


def kernel(
    n_lat, n_lon, rank,
    mean_ref, fac_ref, depth_ref, cells_ref, count_ref, vals_ref, err_ref,
    upd_ref, out_ref,
    up_buf, dn_buf, aux, aux_up, aux_dn, edge_right, edge_left, from_left, from_right,
    fc, gt, p1, p2, ar1, ar2,
    s_main, r_main, s_aux, r_aux, s_el, r_el, s_er, r_er, s1, r1, s2, r2,
):
    lat, lon = lax.axis_index("lat"), lax.axis_index("lon")
    band, lanes = depth_ref.shape
    groups = rank // T
    slot = lanes // groups
    half_slot = slot // 2
    edge = 2 * STEPS
    per = 3 * band
    chunk = T * per
    lane8 = lax.broadcasted_iota(jnp.int32, (T, lanes), 1)
    sub8 = lax.broadcasted_iota(jnp.int32, (T, lanes), 0)

    def at(dlat, dlon):
        return (lax.rem(lat + dlat + n_lat, n_lat), lax.rem(lon + dlon + n_lon, n_lon))

    diagonals = [(a, b) for a in (-1, 1) for b in (-1, 1)]
    peers = [(a, 0) for a in range(1, n_lat)] + [(0, b) for b in range(1, n_lon)] + diagonals
    barrier = pltpu.get_barrier_semaphore()
    for a, b in peers:
        pl.semaphore_signal(barrier, inc=1, device_id=at(a, b), device_id_type=MESH)

    has_up, has_dn = lat > 0, lat < n_lat - 1
    aux[0 : 3 * band, :] = mean_ref[...]
    aux[3 * band :, :] = depth_ref[...]

    @pl.when(jnp.logical_not(has_up))
    def _():
        up_buf[...] = jnp.zeros_like(up_buf)
        aux_up[...] = jnp.zeros_like(aux_up)
        from_left[0] = jnp.zeros_like(from_left[0])
        from_right[0] = jnp.zeros_like(from_right[0])

    @pl.when(jnp.logical_not(has_dn))
    def _():
        dn_buf[...] = jnp.zeros_like(dn_buf)
        aux_dn[...] = jnp.zeros_like(aux_dn)
        from_left[2] = jnp.zeros_like(from_left[2])
        from_right[2] = jnp.zeros_like(from_right[2])

    def remote(src, dst, ssem, rsem, where):
        return pltpu.make_async_remote_copy(
            src_ref=src, dst_ref=dst, send_sem=ssem, recv_sem=rsem, device_id=where, device_id_type=MESH
        )

    def main_copy(side, g):
        rows = pl.ds(g * chunk, chunk)
        dst = (up_buf, dn_buf)[side]
        return remote(fac_ref.at[rows], dst.at[rows], s_main.at[side, g], r_main.at[side, g], at(1 - 2 * side, 0))

    def aux_copy(side):
        dst = (aux_up, aux_dn)[side]
        return remote(aux, dst, s_aux.at[side], r_aux.at[side], at(1 - 2 * side, 0))

    def edge_copy(to_right, block):
        dlat = 1 - block
        if to_right:
            return remote(edge_right, from_left.at[block], s_er.at[block], r_er.at[block], at(dlat, 1))
        return remote(edge_left, from_right.at[block], s_el.at[block], r_el.at[block], at(dlat, -1))

    sends = (has_dn, has_up)
    receives = (has_up, has_dn)

    pl.semaphore_wait(barrier, len(peers))
    for side in range(2):
        @pl.when(sends[side])
        def _(side=side):
            aux_copy(side).start()
            for g in range(groups):
                main_copy(side, g).start()

    def load(ref, f, g):
        return jnp.concatenate([ref[pl.ds(g * chunk + f * band + r, T, stride=per), :] for r in range(band)], 0)

    stack_lane = lax.broadcasted_iota(jnp.int32, (T * band, lanes), 1)
    stack_sub = lax.broadcasted_iota(jnp.int32, (T * band, lanes), 0)

    def seam_tiles(ref, f):
        tiles = roll(load(ref, f, groups - 1), slot * (groups - 1) + half_slot)
        for g in range(groups - 1):
            tiles = jnp.where(
                (stack_lane >= slot * g) & (stack_lane < slot * (g + 1)),
                roll(load(ref, f, g), slot * g + half_slot),
                tiles,
            )
        return tiles

    fold = slot // edge
    own_seams = []
    tiles_per = band // fold
    in_slot = lax.rem(lane8, slot)
    for f in range(3):
        seams = seam_tiles(fac_ref, f)
        own_seams.append(seams)
        for t in range(tiles_per):
            right = left = None
            for q in range(fold):
                tile = seams[T * (t * fold + q) : T * (t * fold + q + 1)]
                to_right = roll(tile, edge * q - (half_slot - edge))
                to_left = roll(tile, edge * q - half_slot)
                keep = (in_slot >= edge * q) & (in_slot < edge * (q + 1))
                right = to_right if q == 0 else jnp.where(keep, to_right, right)
                left = to_left if q == 0 else jnp.where(keep, to_left, left)
            row = T * (f * tiles_per + t)
            edge_right[row : row + T, :] = right
            edge_left[row : row + T, :] = left
    aux_edge = None
    for f in range(4):
        tile = roll(aux[f * band : (f + 1) * band, :], 2 * edge * f + edge)
        aux_edge = tile if f == 0 else jnp.where(lane8 >= 2 * edge * f, tile, aux_edge)
    edge_rows = T * 3 * tiles_per
    edge_right[edge_rows:, :] = aux_edge
    edge_left[edge_rows:, :] = aux_edge

    for block in (1, 0, 2):
        def go(block=block):
            edge_copy(True, block).start()
            edge_copy(False, block).start()
        if block == 1:
            go()
        else:
            pl.when(sends[0] if block == 0 else sends[1])(go)

    cells = cells_ref[...]
    slots = cells.shape[1]
    live = lax.broadcasted_iota(jnp.int32, (1, slots), 1) < count_ref[...]
    weight = jnp.where(live, 1.0, 0.0) / err_ref[...]
    square = weight * weight
    obs_row = jnp.zeros_like(cells)
    for r in range(1, band):
        obs_row = obs_row + jnp.where(cells >= r * lanes, 1, 0)
    obs_col = cells - lanes * obs_row
    row_hot = lax.broadcasted_iota(jnp.int32, (band, slots), 0) == obs_row
    left_side = jnp.concatenate(
        [jnp.where(row_hot, square, 0.0), jnp.where(row_hot, square * vals_ref[...], 0.0)], 0
    )
    col_hot = jnp.where(lax.broadcasted_iota(jnp.int32, (lanes, slots), 0) == obs_col, 1.0, 0.0)
    cell_sums = lax.dot_general(left_side, col_hot, NT, precision=HIGHEST, preferred_element_type=jnp.float32)
    cell_weight, cell_value = cell_sums[:band], cell_sums[band:]

    half = 0.5 * TIME_STEP
    up_gain = jnp.where(has_up, half, 0.0).astype(jnp.float32)
    down_gain = jnp.where(has_dn, half, 0.0).astype(jnp.float32)

    def spread(tile):
        return jnp.concatenate([jnp.broadcast_to(tile[r : r + 1], (T, lanes)) for r in range(band)], 0)

    for side in range(2):
        @pl.when(receives[side])
        def _(side=side):
            aux_copy(side).wait_recv()
    aux_blocks = (aux_up, aux, aux_dn)
    coef = jnp.concatenate([half * spread(b[3 * band :, :]) for b in aux_blocks], 0)

    blocks = (up_buf, fac_ref, dn_buf)
    for g in range(groups):
        for side in range(2):
            @pl.when(receives[side])
            def _(side=side, g=g):
                main_copy(side, g).wait_recv()
        state = [jnp.concatenate([load(b, f, g) for b in blocks], 0) for f in range(3)]
        state = evolve(*state, coef, up_gain, down_gain, band)
        for f in range(3):
            for r in range(band):
                fc[f * band + r, T * g : T * (g + 1), :] = state[f][T * r : T * (r + 1)]

    edge_copy(True, 1).wait_recv()
    edge_copy(False, 1).wait_recv()
    for side in range(2):
        @pl.when(receives[side])
        def _(side=side):
            edge_copy(True, 2 * side).wait_recv()
            edge_copy(False, 2 * side).wait_recv()

    def aux_pair(b, f):
        own = aux_blocks[b][f * band : (f + 1) * band, :]
        left = from_left[b, edge_rows:, :]
        right = from_right[b, edge_rows:, :]
        strips = jnp.where(lane8 < half_slot, roll(left, half_slot - edge - 2 * edge * f), roll(own, half_slot))
        strips = jnp.where(
            lane8 < slot,
            strips,
            jnp.where(lane8 < slot + half_slot, roll(own, slot + half_slot), roll(right, slot + half_slot - edge - 2 * edge * f)),
        )
        return own, strips

    def mean_group(b, f):
        own, strips = aux_pair(b, f)
        return jnp.concatenate([jnp.where(sub8 == 0, own[r : r + 1], strips[r : r + 1]) for r in range(band)], 0)

    mean_state = [jnp.concatenate([mean_group(b, f) for b in range(3)], 0) for f in range(4)]
    mean_state = evolve(*mean_state[:3], half * mean_state[3], up_gain, down_gain, band)
    mean = []
    for f in range(3):
        strips = roll(mean_state[f], -1, 0)
        low = roll(strips, -half_slot)
        high = roll(strips, lanes - half_slot - slot)
        mean.append(jnp.where(stack_lane < edge, low, jnp.where(stack_lane >= lanes - edge, high, mean_state[f])))

    def repeat_slots(tile):
        tile = jnp.where(lane8 < slot, tile, 0.0)
        total = tile
        for g in range(1, groups):
            total = total + roll(tile, slot * g)
        return total

    strips_of = [aux_pair(b, 3)[1] for b in range(3)]
    coef_left = jnp.concatenate([half * spread(repeat_slots(s)) for s in strips_of], 0)
    coef_right = jnp.concatenate([half * spread(repeat_slots(roll(s, -slot))) for s in strips_of], 0)

    def unpack(ref, b, f, first):
        out = []
        for r in range(band):
            row = T * (f * tiles_per + r // fold)
            out.append(roll(ref[b, row : row + T, :], first - edge * (r % fold)))
        return jnp.concatenate(out, 0)

    low_half = lax.rem(stack_lane, slot) < half_slot
    left_state, right_state = [], []
    for f in range(3):
        lefts, rights = [], []
        for b in range(3):
            seams = own_seams[f] if b == 1 else seam_tiles(blocks[b], f)
            lefts.append(jnp.where(low_half, unpack(from_left, b, f, half_slot - edge), seams))
            rights.append(jnp.where(low_half, seams, unpack(from_right, b, f, half_slot)))
        left_state.append(jnp.concatenate(lefts, 0))
        right_state.append(jnp.concatenate(rights, 0))
    left_state = evolve(*left_state, coef_left, up_gain, down_gain, band)
    right_state = evolve(*right_state, coef_right, up_gain, down_gain, band)
    at_edge = (lane8 < edge) | (lane8 >= lanes - edge)
    for f in range(3):
        seams = jnp.where(low_half, right_state[f], left_state[f])
        for g in range(groups):
            back = roll(seams, -(slot * g + half_slot))
            for r in range(band):
                spot = (f * band + r, slice(T * g, T * (g + 1)), slice(None))
                fc[spot] = jnp.where(at_edge, back[T * r : T * (r + 1)], fc[spot])

    lhs, rhs = [], []
    for r in range(band):
        height = fc[r]
        w = cell_weight[r : r + 1]
        drive = cell_value[r : r + 1] - w * mean[0][T * r : T * r + 1]
        lhs.append(height)
        rhs.append(jnp.concatenate([height * w, jnp.where(sub8 == 0, drive, 0.0)], 0))
    gram = lax.dot_general(
        jnp.concatenate(lhs, 1), jnp.concatenate(rhs, 1), NT, precision=HIGHEST, preferred_element_type=jnp.float32
    )
    gt[...] = jnp.zeros_like(gt)
    gt[:, 0 : rank + T] = gram
    hr = rank // 2
    wide = lax.broadcasted_iota(jnp.int32, (hr, lanes), 1)
    mine = jnp.where(wide < lanes // 2, gt[0:hr, :], roll(gt[hr:, :], lanes // 2))

    p1[...] = mine
    def lat_copy(o):
        return remote(p1, ar1.at[o - 1], s1.at[o - 1], r1.at[o - 1], at(o, 0))
    def lon_copy(o):
        return remote(p2, ar2.at[o - 1], s2.at[o - 1], r2.at[o - 1], at(0, o))
    for o in range(1, n_lat):
        lat_copy(o).start()
    for o in range(1, n_lat):
        lat_copy(o).wait_recv()
        mine = mine + ar1[o - 1]
    p2[...] = mine
    for o in range(1, n_lon):
        lon_copy(o).start()
    for o in range(1, n_lon):
        lon_copy(o).wait_recv()
        mine = mine + ar2[o - 1]

    both = jnp.concatenate([mine, roll(mine, lanes // 2)], 0)
    ri = lax.broadcasted_iota(jnp.int32, (rank, lanes), 0)
    li = lax.broadcasted_iota(jnp.int32, (rank, lanes), 1)
    eyes = jnp.where((li == ri) | (li == ri + lanes // 2), 1.0, 0.0)
    x = jnp.where(li < lanes // 2, both, 0.0) + eyes
    tiles = [x[T * i : T * (i + 1)] for i in range(groups)]
    for j in range(rank):
        tj, sj = j // T, j % T
        row = tiles[tj][sj : sj + 1]
        inv = 1.0 / row[:, j : j + 1]
        scaled_row = row * inv
        for i in range(tj, groups):
            if i == tj and sj == T - 1:
                continue
            col = tiles[i][:, j : j + 1]
            if i == tj:
                col = jnp.where(sub8[:, :1] > sj, col, 0.0)
            tiles[i] = tiles[i] - col * scaled_row
    x = jnp.concatenate(tiles, 0)
    pivot = jnp.sum(jnp.where(li == ri, x, 0.0), 1, keepdims=True)
    x = x / jnp.sqrt(pivot)
    inverse = jnp.where(li < rank, roll(x, -(lanes // 2)), 0.0)
    z = x[:, rank : rank + 1]
    shift = jnp.sum(inverse * z, 0, keepdims=True)
    coefs = jnp.concatenate([inverse, jnp.where(sub8 == 0, shift, 0.0)], 0)[:, :rank]

    for f in range(3):
        slab = jnp.concatenate([fc[f * band + r] for r in range(band)], 1)
        res = jnp.dot(coefs, slab, precision=HIGHEST, preferred_element_type=jnp.float32)
        for r in range(band):
            part = res[:, lanes * r : lanes * (r + 1)]
            i = f * band + r
            for g in range(groups):
                out_ref[pl.ds(g * chunk + i, T, stride=per), :] = part[T * g : T * (g + 1)]
            upd_ref[i : i + 1, :] = mean[f][T * r : T * r + 1] + part[rank : rank + 1]

    for side in range(2):
        @pl.when(sends[side])
        def _(side=side):
            aux_copy(side).wait_send()
            for g in range(groups):
                main_copy(side, g).wait_send()
            edge_copy(True, 2 * side).wait_send()
            edge_copy(False, 2 * side).wait_send()
    edge_copy(True, 1).wait_send()
    edge_copy(False, 1).wait_send()
    for o in range(1, n_lat):
        lat_copy(o).wait_send()
    for o in range(1, n_lon):
        lon_copy(o).wait_send()


def per_device(n_lat, n_lon, background, factor, depth, cells, count, values, error):
    rank, fields, band, lanes = factor.shape
    groups = rank // T
    rows = rank * fields * band
    slots = cells.shape[0]
    assert band == T and 2 * STEPS <= band and rank % T == 0 and fields == 3
    edge_rows = T * (fields * band * groups * 2 * STEPS // lanes + 1)
    vmem = pl.BlockSpec(memory_space=pltpu.VMEM)
    f32 = functools.partial(pltpu.VMEM, dtype=jnp.float32)
    dma = pltpu.SemaphoreType.DMA
    updated, analysis = pl.pallas_call(
        functools.partial(kernel, n_lat, n_lon, rank),
        out_shape=(
            jax.ShapeDtypeStruct((fields * band, lanes), jnp.float32),
            jax.ShapeDtypeStruct((rows, lanes), jnp.float32),
        ),
        in_specs=[vmem] * 7,
        out_specs=(vmem, vmem),
        scratch_shapes=[
            f32((rows, lanes)), f32((rows, lanes)),
            f32((4 * band, lanes)), f32((4 * band, lanes)), f32((4 * band, lanes)),
            f32((edge_rows, lanes)), f32((edge_rows, lanes)),
            f32((3, edge_rows, lanes)), f32((3, edge_rows, lanes)),
            f32((fields * band, rank, lanes)), f32((rank, lanes)),
            f32((rank // 2, lanes)), f32((rank // 2, lanes)),
            f32((n_lat - 1, rank // 2, lanes)), f32((n_lon - 1, rank // 2, lanes)),
            dma((2, groups)), dma((2, groups)), dma((2,)), dma((2,)),
            dma((3,)), dma((3,)), dma((3,)), dma((3,)),
            dma((n_lat - 1,)), dma((n_lat - 1,)), dma((n_lon - 1,)), dma((n_lon - 1,)),
        ],
        compiler_params=pltpu.CompilerParams(
            collective_id=0, has_side_effects=True, vmem_limit_bytes=32 * 1024 * 1024
        ),
    )(
        background.reshape(fields * band, lanes), factor.reshape(rows, lanes), depth,
        cells.reshape(1, slots), count.reshape(1, 1), values.reshape(1, slots), error.reshape(1, slots),
    )
    return updated.reshape(background.shape), analysis.reshape(factor.shape)


def solution(mesh):
    return jax.shard_map(
        functools.partial(per_device, mesh.shape["lat"], mesh.shape["lon"]),
        mesh=mesh,
        in_specs=(
            P(None, "lat", "lon"),
            P(None, None, "lat", "lon"),
            P("lat", "lon"),
            P(("lat", "lon")),
            P(("lat", "lon")),
            P(("lat", "lon")),
            P(("lat", "lon")),
        ),
        out_specs=(P(None, "lat", "lon"), P(None, None, "lat", "lon")),
        check_vma=False,
    )
```

```python
import functools

import jax
import jax.numpy as jnp
from jax import lax
from jax.experimental import pallas as pl
from jax.experimental.pallas import tpu as pltpu
from jax.sharding import PartitionSpec as P

STEPS = 4
TIME_STEP = 0.9
ROTATION = 0.25
MESH = pl.DeviceIdType.MESH
T = 8
NT = (((1,), (1,)), ((), ()))


def roll(x, shift, axis=1):
    shift = shift % x.shape[axis]
    return x if shift == 0 else pltpu.roll(x, shift, axis)


def split(x, terms):
    parts = []
    for _ in range(terms):
        part = x.astype(jnp.bfloat16)
        parts.append(part)
        x = x - part.astype(jnp.float32)
    return parts


def evolve(h, e, n, coef, up_gain, down_gain, band):
    half = 0.5 * TIME_STEP
    for step in range(STEPS):
        w = 2 * (STEPS - step)
        last = coef.shape[0] - T * (band - w + 1)
        mid = e[T:-T]
        div = (roll(mid, -1) - roll(mid, 1)) + (n[2 * T :] - n[: -2 * T])
        hn = h[T:-T] - coef[T * (band - w + 1) : last] * div
        inner = hn[T:-T]
        shape = (T * (w - 2), h.shape[1])
        parts = [jnp.full((T * band, h.shape[1]), half, jnp.float32)]
        if w > 2:
            parts = [jnp.full(shape, up_gain)] + parts + [jnp.full(shape, down_gain)]
        gain = jnp.concatenate(parts, 0) if w > 2 else parts[0]
        e0, n0 = e[2 * T : -2 * T], n[2 * T : -2 * T]
        e = e0 - half * (roll(inner, -1) - roll(inner, 1)) + ROTATION * n0
        n = n0 - gain * (hn[2 * T :] - hn[: -2 * T]) - ROTATION * e0
        h = inner
    return h, e, n


def kernel(
    n_lat, n_lon, rank,
    mean_hbm, fac_hbm, depth_hbm, cells_hbm, count_hbm, vals_hbm, err_hbm,
    fc, mean_out, gram_out,
    fac_ref, cells_ref, count_ref, vals_ref, err_ref, s_in,
    up_buf, dn_buf, aux, aux_up, aux_dn, edge_right, edge_left, from_left, from_right,
    p1, p2, ar1, ar2,
    s_main, r_main, s_aux, r_aux, s_el, r_el, s_er, r_er, s1, r1, s2, r2,
):
    lat, lon = lax.axis_index("lat"), lax.axis_index("lon")
    band, lanes = depth_hbm.shape
    groups = rank // T
    slot = lanes // groups
    half_slot = slot // 2
    edge = 2 * STEPS
    per = 3 * band
    chunk = T * per
    lane8 = lax.broadcasted_iota(jnp.int32, (T, lanes), 1)
    sub8 = lax.broadcasted_iota(jnp.int32, (T, lanes), 0)

    def at(dlat, dlon):
        return (lax.rem(lat + dlat + n_lat, n_lat), lax.rem(lon + dlon + n_lon, n_lon))

    diagonals = [(a, b) for a in (-1, 1) for b in (-1, 1)]
    peers = [(a, 0) for a in range(1, n_lat)] + [(0, b) for b in range(1, n_lon)] + diagonals
    barrier = pltpu.get_barrier_semaphore()
    for a, b in peers:
        pl.semaphore_signal(barrier, inc=1, device_id=at(a, b), device_id_type=MESH)

    has_up, has_dn = lat > 0, lat < n_lat - 1
    fetched = [
        pltpu.make_async_copy(src, dst, s_in.at[i])
        for i, (src, dst) in enumerate((
            (mean_hbm, aux.at[pl.ds(0, 3 * band)]),
            (depth_hbm, aux.at[pl.ds(3 * band, band)]),
            (fac_hbm, fac_ref),
            (cells_hbm, cells_ref),
            (count_hbm, count_ref),
            (vals_hbm, vals_ref),
            (err_hbm, err_ref),
        ))
    ]
    for copy in fetched:
        copy.start()

    @pl.when(jnp.logical_not(has_up))
    def _():
        up_buf[...] = jnp.zeros_like(up_buf)
        aux_up[...] = jnp.zeros_like(aux_up)
        from_left[0] = jnp.zeros_like(from_left[0])
        from_right[0] = jnp.zeros_like(from_right[0])

    @pl.when(jnp.logical_not(has_dn))
    def _():
        dn_buf[...] = jnp.zeros_like(dn_buf)
        aux_dn[...] = jnp.zeros_like(aux_dn)
        from_left[2] = jnp.zeros_like(from_left[2])
        from_right[2] = jnp.zeros_like(from_right[2])

    def remote(src, dst, ssem, rsem, where):
        return pltpu.make_async_remote_copy(
            src_ref=src, dst_ref=dst, send_sem=ssem, recv_sem=rsem, device_id=where, device_id_type=MESH
        )

    def main_copy(side, g):
        rows = pl.ds(g * chunk, chunk)
        dst = (up_buf, dn_buf)[side]
        return remote(fac_hbm.at[rows], dst.at[rows], s_main.at[side, g], r_main.at[side, g], at(1 - 2 * side, 0))

    def aux_copy(side):
        dst = (aux_up, aux_dn)[side]
        return remote(aux, dst, s_aux.at[side], r_aux.at[side], at(1 - 2 * side, 0))

    def edge_copy(to_right, block):
        dlat = 1 - block
        if to_right:
            return remote(edge_right, from_left.at[block], s_er.at[block], r_er.at[block], at(dlat, 1))
        return remote(edge_left, from_right.at[block], s_el.at[block], r_el.at[block], at(dlat, -1))

    sends = (has_dn, has_up)
    receives = (has_up, has_dn)

    pl.semaphore_wait(barrier, len(peers))
    fetched[0].wait()
    fetched[1].wait()
    for side in range(2):
        @pl.when(sends[side])
        def _(side=side):
            aux_copy(side).start()
            for g in range(groups):
                main_copy(side, g).start()

    def load(ref, f, g):
        return jnp.concatenate([ref[pl.ds(g * chunk + f * band + r, T, stride=per), :] for r in range(band)], 0)

    stack_lane = lax.broadcasted_iota(jnp.int32, (T * band, lanes), 1)
    stack_sub = lax.broadcasted_iota(jnp.int32, (T * band, lanes), 0)

    def seam_tiles(ref, f):
        tiles = roll(load(ref, f, groups - 1), slot * (groups - 1) + half_slot)
        for g in range(groups - 1):
            tiles = jnp.where(
                (stack_lane >= slot * g) & (stack_lane < slot * (g + 1)),
                roll(load(ref, f, g), slot * g + half_slot),
                tiles,
            )
        return tiles

    fetched[2].wait()
    fold = slot // edge
    own_seams = []
    tiles_per = band // fold
    in_slot = lax.rem(lane8, slot)
    for f in range(3):
        seams = seam_tiles(fac_ref, f)
        own_seams.append(seams)
        for t in range(tiles_per):
            right = left = None
            for q in range(fold):
                tile = seams[T * (t * fold + q) : T * (t * fold + q + 1)]
                to_right = roll(tile, edge * q - (half_slot - edge))
                to_left = roll(tile, edge * q - half_slot)
                keep = (in_slot >= edge * q) & (in_slot < edge * (q + 1))
                right = to_right if q == 0 else jnp.where(keep, to_right, right)
                left = to_left if q == 0 else jnp.where(keep, to_left, left)
            row = T * (f * tiles_per + t)
            edge_right[row : row + T, :] = right
            edge_left[row : row + T, :] = left
    aux_edge = None
    for f in range(4):
        tile = roll(aux[f * band : (f + 1) * band, :], 2 * edge * f + edge)
        aux_edge = tile if f == 0 else jnp.where(lane8 >= 2 * edge * f, tile, aux_edge)
    edge_rows = T * 3 * tiles_per
    edge_right[edge_rows:, :] = aux_edge
    edge_left[edge_rows:, :] = aux_edge

    for block in (1, 0, 2):
        def go(block=block):
            edge_copy(True, block).start()
            edge_copy(False, block).start()
        if block == 1:
            go()
        else:
            pl.when(sends[0] if block == 0 else sends[1])(go)

    for copy in fetched[3:]:
        copy.wait()
    cells = cells_ref[...]
    slots = cells.shape[1]
    live = lax.broadcasted_iota(jnp.int32, (1, slots), 1) < count_ref[...]
    weight = jnp.where(live, 1.0, 0.0) / err_ref[...]
    square = weight * weight
    obs_row = jnp.zeros_like(cells)
    for r in range(1, band):
        obs_row = obs_row + jnp.where(cells >= r * lanes, 1, 0)
    obs_col = cells - lanes * obs_row
    row_hot = lax.broadcasted_iota(jnp.int32, (band, slots), 0) == obs_row
    sums = jnp.concatenate(
        [jnp.where(row_hot, square, 0.0), jnp.where(row_hot, square * vals_ref[...], 0.0)], 0
    )
    col_hot = jnp.where(lax.broadcasted_iota(jnp.int32, (lanes, slots), 0) == obs_col, 1.0, 0.0)
    sums = lax.dot_general(
        jnp.concatenate(split(sums, 3), 0), col_hot.astype(jnp.bfloat16), NT, preferred_element_type=jnp.float32
    )
    sums = (sums[4 * band :] + sums[2 * band : 4 * band]) + sums[: 2 * band]
    cell_weight, cell_value = sums[:band], sums[band:]

    half = 0.5 * TIME_STEP
    up_gain = jnp.where(has_up, half, 0.0).astype(jnp.float32)
    down_gain = jnp.where(has_dn, half, 0.0).astype(jnp.float32)

    def spread(tile):
        return jnp.concatenate([jnp.broadcast_to(tile[r : r + 1], (T, lanes)) for r in range(band)], 0)

    for side in range(2):
        @pl.when(receives[side])
        def _(side=side):
            aux_copy(side).wait_recv()
    aux_blocks = (aux_up, aux, aux_dn)
    coef = jnp.concatenate([half * spread(b[3 * band :, :]) for b in aux_blocks], 0)

    blocks = (up_buf, fac_ref, dn_buf)
    for g in range(groups):
        for side in range(2):
            @pl.when(receives[side])
            def _(side=side, g=g):
                main_copy(side, g).wait_recv()
        state = [jnp.concatenate([load(b, f, g) for b in blocks], 0) for f in range(3)]
        state = evolve(*state, coef, up_gain, down_gain, band)
        for f in range(3):
            for r in range(band):
                fc[f * band + r, T * g : T * (g + 1), :] = state[f][T * r : T * (r + 1)]

    edge_copy(True, 1).wait_recv()
    edge_copy(False, 1).wait_recv()
    for side in range(2):
        @pl.when(receives[side])
        def _(side=side):
            edge_copy(True, 2 * side).wait_recv()
            edge_copy(False, 2 * side).wait_recv()

    def aux_pair(b, f):
        own = aux_blocks[b][f * band : (f + 1) * band, :]
        left = from_left[b, edge_rows:, :]
        right = from_right[b, edge_rows:, :]
        strips = jnp.where(lane8 < half_slot, roll(left, half_slot - edge - 2 * edge * f), roll(own, half_slot))
        strips = jnp.where(
            lane8 < slot,
            strips,
            jnp.where(lane8 < slot + half_slot, roll(own, slot + half_slot), roll(right, slot + half_slot - edge - 2 * edge * f)),
        )
        return own, strips

    def mean_group(b, f):
        own, strips = aux_pair(b, f)
        return jnp.concatenate([jnp.where(sub8 == 0, own[r : r + 1], strips[r : r + 1]) for r in range(band)], 0)

    mean_state = [jnp.concatenate([mean_group(b, f) for b in range(3)], 0) for f in range(4)]
    mean_state = evolve(*mean_state[:3], half * mean_state[3], up_gain, down_gain, band)
    mean = []
    for f in range(3):
        strips = roll(mean_state[f], -1, 0)
        low = roll(strips, -half_slot)
        high = roll(strips, lanes - half_slot - slot)
        mean.append(jnp.where(stack_lane < edge, low, jnp.where(stack_lane >= lanes - edge, high, mean_state[f])))

    def repeat_slots(tile):
        tile = jnp.where(lane8 < slot, tile, 0.0)
        total = tile
        for g in range(1, groups):
            total = total + roll(tile, slot * g)
        return total

    strips_of = [aux_pair(b, 3)[1] for b in range(3)]
    coef_left = jnp.concatenate([half * spread(repeat_slots(s)) for s in strips_of], 0)
    coef_right = jnp.concatenate([half * spread(repeat_slots(roll(s, -slot))) for s in strips_of], 0)

    def unpack(ref, b, f, first):
        out = []
        for r in range(band):
            row = T * (f * tiles_per + r // fold)
            out.append(roll(ref[b, row : row + T, :], first - edge * (r % fold)))
        return jnp.concatenate(out, 0)

    low_half = lax.rem(stack_lane, slot) < half_slot
    left_state, right_state = [], []
    for f in range(3):
        lefts, rights = [], []
        for b in range(3):
            seams = own_seams[f] if b == 1 else seam_tiles(blocks[b], f)
            lefts.append(jnp.where(low_half, unpack(from_left, b, f, half_slot - edge), seams))
            rights.append(jnp.where(low_half, seams, unpack(from_right, b, f, half_slot)))
        left_state.append(jnp.concatenate(lefts, 0))
        right_state.append(jnp.concatenate(rights, 0))
    left_state = evolve(*left_state, coef_left, up_gain, down_gain, band)
    right_state = evolve(*right_state, coef_right, up_gain, down_gain, band)
    at_edge = (lane8 < edge) | (lane8 >= lanes - edge)
    for f in range(3):
        seams = jnp.where(low_half, right_state[f], left_state[f])
        for g in range(groups):
            back = roll(seams, -(slot * g + half_slot))
            for r in range(band):
                spot = (f * band + r, slice(T * g, T * (g + 1)), slice(None))
                fc[spot] = jnp.where(at_edge, back[T * r : T * (r + 1)], fc[spot])

    for f in range(3):
        for r in range(band):
            mean_out[f * band + r : f * band + r + 1, :] = mean[f][T * r : T * r + 1]

    lhs, rhs = [], []
    for r in range(band):
        height = fc[r]
        w = cell_weight[r : r + 1]
        drive = cell_value[r : r + 1] - w * mean[0][T * r : T * r + 1]
        lhs.append(height)
        pad = jnp.zeros((lanes // 2 - rank - T, lanes), jnp.float32)
        rhs.append(jnp.concatenate([height * w, jnp.where(sub8 == 0, drive, 0.0), pad], 0))
    gram = lax.dot_general(
        jnp.concatenate(split(jnp.concatenate(lhs, 1), 2), 0),
        jnp.concatenate(split(jnp.concatenate(rhs, 1), 2), 0),
        NT, preferred_element_type=jnp.float32,
    )
    gram = gram[:rank] + gram[rank:]
    gram = gram + roll(gram, lanes // 2)
    hr = rank // 2
    wide = lax.broadcasted_iota(jnp.int32, (hr, lanes), 1)
    mine = jnp.where(wide < lanes // 2, gram[:hr], gram[hr:])

    p1[...] = mine
    def lat_copy(o):
        return remote(p1, ar1.at[o - 1], s1.at[o - 1], r1.at[o - 1], at(o, 0))
    def lon_copy(o):
        return remote(p2, ar2.at[o - 1], s2.at[o - 1], r2.at[o - 1], at(0, o))
    for o in range(1, n_lat):
        lat_copy(o).start()
    for o in range(1, n_lat):
        lat_copy(o).wait_recv()
        mine = mine + ar1[o - 1]
    p2[...] = mine
    for o in range(1, n_lon):
        lon_copy(o).start()
    for o in range(1, n_lon):
        lon_copy(o).wait_recv()
        mine = mine + ar2[o - 1]

    gram_out[...] = mine

    for side in range(2):
        @pl.when(sends[side])
        def _(side=side):
            aux_copy(side).wait_send()
            for g in range(groups):
                main_copy(side, g).wait_send()
            edge_copy(True, 2 * side).wait_send()
            edge_copy(False, 2 * side).wait_send()
    edge_copy(True, 1).wait_send()
    edge_copy(False, 1).wait_send()
    for o in range(1, n_lat):
        lat_copy(o).wait_send()
    for o in range(1, n_lon):
        lon_copy(o).wait_send()


def transform(rank, fc, mean_ref, gram_ref, upd_hbm, out_hbm, upd, res, s_out):
    mine = gram_ref[...]
    lanes = mine.shape[1]
    band = fc.shape[0] // 3
    groups = rank // T
    sub8 = lax.broadcasted_iota(jnp.int32, (T, lanes), 0)
    both = jnp.concatenate([mine, roll(mine, lanes // 2)], 0)
    ri = lax.broadcasted_iota(jnp.int32, (rank, lanes), 0)
    li = lax.broadcasted_iota(jnp.int32, (rank, lanes), 1)
    eyes = jnp.where((li == ri) | (li == ri + lanes // 2), 1.0, 0.0)
    x = jnp.where(li < lanes // 2, both, 0.0) + eyes
    tiles = [x[T * i : T * (i + 1)] for i in range(groups)]
    for b in range(groups):
        cols = {
            (i, q): jnp.broadcast_to(tiles[i][:, T * b + q : T * b + q + 1], (T, lanes))
            for i in range(b, groups)
            for q in range(T)
        }
        for q in range(T):
            inv = 1.0 / cols[b, q][q : q + 1]
            row = tiles[b][q : q + 1]
            heads = [cols[b, p][q : q + 1] for p in range(q + 1, T)]
            for i in range(b, groups):
                if i == b and q == T - 1:
                    continue
                m = cols[i, q] * inv
                if i == b:
                    m = jnp.where(sub8 > q, m, 0.0)
                for p in range(q + 1, T):
                    cols[i, p] = cols[i, p] - m * heads[p - q - 1]
                tiles[i] = tiles[i] - m * row
    x = jnp.concatenate(tiles, 0)
    pivot = jnp.sum(jnp.where(li == ri, x, 0.0), 1, keepdims=True)
    x = x / jnp.sqrt(pivot)
    inverse = jnp.where(li < rank, roll(x, -(lanes // 2)), 0.0)
    z = x[:, rank : rank + 1]
    shift = jnp.sum(inverse * z, 0, keepdims=True)
    coefs = jnp.concatenate([inverse, jnp.where(sub8 == 0, shift, 0.0)], 0)
    high, low = (c.astype(jnp.float32) for c in split(coefs, 2))
    stacked = (high + roll(high, rank) + roll(low, 2 * rank))[:, : 3 * rank].astype(jnp.bfloat16)

    per = 3 * band
    for f in range(3):
        slab = jnp.concatenate([fc[f * band + r] for r in range(band)], 1)
        high, low = split(slab, 2)
        part = jnp.dot(stacked, jnp.concatenate([high, low, high], 0), preferred_element_type=jnp.float32)
        for r in range(band):
            col = part[:, lanes * r : lanes * (r + 1)]
            i = f * band + r
            for g in range(groups):
                res[pl.ds(g * T * per + i, T, stride=per), :] = col[T * g : T * (g + 1)]
            upd[i : i + 1, :] = mean_ref[i : i + 1, :] + col[rank : rank + 1]
    copies = [
        pltpu.make_async_copy(res, out_hbm, s_out.at[0]),
        pltpu.make_async_copy(upd, upd_hbm, s_out.at[1]),
    ]
    for copy in copies:
        copy.start()
    for copy in copies:
        copy.wait()


def in_hbm(x):
    return pltpu.with_memory_space_constraint(x, pltpu.HBM)


def per_device(n_lat, n_lon, background, factor, depth, cells, count, values, error):
    rank, fields, band, lanes = factor.shape
    groups = rank // T
    rows = rank * fields * band
    slots = cells.shape[0]
    assert band == T and 2 * STEPS <= band and rank % T == 0 and fields == 3
    edge_rows = T * (fields * band * groups * 2 * STEPS // lanes + 1)
    vmem = pl.BlockSpec(memory_space=pltpu.VMEM)
    f32 = functools.partial(pltpu.VMEM, dtype=jnp.float32)
    dma = pltpu.SemaphoreType.DMA
    anywhere = pl.BlockSpec(memory_space=pl.ANY)
    forecast, mean, gram = pl.pallas_call(
        functools.partial(kernel, n_lat, n_lon, rank),
        out_shape=(
            jax.ShapeDtypeStruct((fields * band, rank, lanes), jnp.float32),
            jax.ShapeDtypeStruct((fields * band, lanes), jnp.float32),
            jax.ShapeDtypeStruct((rank // 2, lanes), jnp.float32),
        ),
        in_specs=[pl.BlockSpec(memory_space=pltpu.HBM)] * 7,
        out_specs=(vmem, vmem, vmem),
        scratch_shapes=[
            f32((rows, lanes)), pltpu.VMEM((1, slots), jnp.int32), pltpu.VMEM((1, 1), jnp.int32),
            f32((1, slots)), f32((1, slots)), dma((7,)),
            f32((rows, lanes)), f32((rows, lanes)),
            f32((4 * band, lanes)), f32((4 * band, lanes)), f32((4 * band, lanes)),
            f32((edge_rows, lanes)), f32((edge_rows, lanes)),
            f32((3, edge_rows, lanes)), f32((3, edge_rows, lanes)),
            f32((rank // 2, lanes)), f32((rank // 2, lanes)),
            f32((n_lat - 1, rank // 2, lanes)), f32((n_lon - 1, rank // 2, lanes)),
            dma((2, groups)), dma((2, groups)), dma((2,)), dma((2,)),
            dma((3,)), dma((3,)), dma((3,)), dma((3,)),
            dma((n_lat - 1,)), dma((n_lat - 1,)), dma((n_lon - 1,)), dma((n_lon - 1,)),
        ],
        compiler_params=pltpu.CompilerParams(
            collective_id=0, has_side_effects=True, vmem_limit_bytes=32 * 1024 * 1024
        ),
    )(
        in_hbm(background.reshape(fields * band, lanes)), in_hbm(factor.reshape(rows, lanes)), in_hbm(depth),
        in_hbm(cells.reshape(1, slots)), count.reshape(1, 1), in_hbm(values.reshape(1, slots)), in_hbm(error.reshape(1, slots)),
    )
    updated, analysis = pl.pallas_call(
        functools.partial(transform, rank),
        out_shape=(
            jax.ShapeDtypeStruct((fields * band, lanes), jnp.float32),
            jax.ShapeDtypeStruct((rows, lanes), jnp.float32),
        ),
        in_specs=[vmem] * 3,
        out_specs=(anywhere, anywhere),
        scratch_shapes=[f32((fields * band, lanes)), f32((rows, lanes)), dma((2,))],
        compiler_params=pltpu.CompilerParams(vmem_limit_bytes=16 * 1024 * 1024),
    )(forecast, mean, gram)
    return updated.reshape(background.shape), analysis.reshape(factor.shape)


def solution(mesh):
    return jax.shard_map(
        functools.partial(per_device, mesh.shape["lat"], mesh.shape["lon"]),
        mesh=mesh,
        in_specs=(
            P(None, "lat", "lon"),
            P(None, None, "lat", "lon"),
            P("lat", "lon"),
            P(("lat", "lon")),
            P(("lat", "lon")),
            P(("lat", "lon")),
            P(("lat", "lon")),
        ),
        out_specs=(P(None, "lat", "lon"), P(None, None, "lat", "lon")),
        check_vma=False,
    )
```

```python
import functools

import jax
import jax.numpy as jnp
from jax import lax
from jax.experimental import pallas as pl
from jax.experimental.pallas import tpu as pltpu
from jax.sharding import PartitionSpec as P

STEPS = 4
TIME_STEP = 0.9
ROTATION = 0.25
MESH = pl.DeviceIdType.MESH
T = 8
NT = (((1,), (1,)), ((), ()))


def roll(x, shift, axis=1):
    shift = shift % x.shape[axis]
    return x if shift == 0 else pltpu.roll(x, shift, axis)


def split(x, terms):
    parts = []
    for _ in range(terms):
        part = x.astype(jnp.bfloat16)
        parts.append(part)
        x = x - part.astype(jnp.float32)
    return parts


def evolve(h, e, n, coef, up_gain, down_gain, band):
    half = 0.5 * TIME_STEP
    for step in range(STEPS):
        w = 2 * (STEPS - step)
        last = coef.shape[0] - T * (band - w + 1)
        mid = e[T:-T]
        div = (roll(mid, -1) - roll(mid, 1)) + (n[2 * T :] - n[: -2 * T])
        hn = h[T:-T] - coef[T * (band - w + 1) : last] * div
        inner = hn[T:-T]
        shape = (T * (w - 2), h.shape[1])
        parts = [jnp.full((T * band, h.shape[1]), half, jnp.float32)]
        if w > 2:
            parts = [jnp.full(shape, up_gain)] + parts + [jnp.full(shape, down_gain)]
        gain = jnp.concatenate(parts, 0) if w > 2 else parts[0]
        e0, n0 = e[2 * T : -2 * T], n[2 * T : -2 * T]
        e = e0 - half * (roll(inner, -1) - roll(inner, 1)) + ROTATION * n0
        n = n0 - gain * (hn[2 * T :] - hn[: -2 * T]) - ROTATION * e0
        h = inner
    return h, e, n


def kernel(
    n_lat, n_lon, rank,
    mean_hbm, fac_hbm, depth_hbm, cells_hbm, count_hbm, vals_hbm, err_hbm,
    fc, mean_out, gram_out,
    fac_ref, cells_ref, count_ref, vals_ref, err_ref, s_in,
    up_buf, dn_buf, aux, aux_up, aux_dn, edge_right, edge_left, from_left, from_right,
    seam_buf, p1, p2, ar1, ar2,
    s_main, r_main, s_aux, r_aux, s_el, r_el, s_er, r_er, s1, r1, s2, r2,
):
    lat, lon = lax.axis_index("lat"), lax.axis_index("lon")
    band, lanes = depth_hbm.shape
    groups = rank // T
    slot = lanes // groups
    half_slot = slot // 2
    edge = 2 * STEPS
    per = 3 * band
    chunk = T * per
    lane8 = lax.broadcasted_iota(jnp.int32, (T, lanes), 1)
    sub8 = lax.broadcasted_iota(jnp.int32, (T, lanes), 0)

    def at(dlat, dlon):
        return (lax.rem(lat + dlat + n_lat, n_lat), lax.rem(lon + dlon + n_lon, n_lon))

    diagonals = [(a, b) for a in (-1, 1) for b in (-1, 1)]
    peers = [(a, 0) for a in range(1, n_lat)] + [(0, b) for b in range(1, n_lon)] + diagonals
    barrier = pltpu.get_barrier_semaphore()
    for a, b in peers:
        pl.semaphore_signal(barrier, inc=1, device_id=at(a, b), device_id_type=MESH)

    has_up, has_dn = lat > 0, lat < n_lat - 1
    fetched = [
        pltpu.make_async_copy(src, dst, s_in.at[i])
        for i, (src, dst) in enumerate((
            (mean_hbm, aux.at[pl.ds(0, 3 * band)]),
            (depth_hbm, aux.at[pl.ds(3 * band, band)]),
            (fac_hbm, fac_ref),
            (cells_hbm, cells_ref),
            (count_hbm, count_ref),
            (vals_hbm, vals_ref),
            (err_hbm, err_ref),
        ))
    ]
    for copy in fetched:
        copy.start()

    @pl.when(jnp.logical_not(has_up))
    def _():
        up_buf[...] = jnp.zeros_like(up_buf)
        aux_up[...] = jnp.zeros_like(aux_up)
        from_left[0] = jnp.zeros_like(from_left[0])
        from_right[0] = jnp.zeros_like(from_right[0])

    @pl.when(jnp.logical_not(has_dn))
    def _():
        dn_buf[...] = jnp.zeros_like(dn_buf)
        aux_dn[...] = jnp.zeros_like(aux_dn)
        from_left[2] = jnp.zeros_like(from_left[2])
        from_right[2] = jnp.zeros_like(from_right[2])

    def remote(src, dst, ssem, rsem, where):
        return pltpu.make_async_remote_copy(
            src_ref=src, dst_ref=dst, send_sem=ssem, recv_sem=rsem, device_id=where, device_id_type=MESH
        )

    def main_copy(side, g):
        rows = pl.ds(g * chunk, chunk)
        dst = (up_buf, dn_buf)[side]
        return remote(fac_hbm.at[rows], dst.at[rows], s_main.at[side, g], r_main.at[side, g], at(1 - 2 * side, 0))

    def aux_copy(side):
        dst = (aux_up, aux_dn)[side]
        return remote(aux, dst, s_aux.at[side], r_aux.at[side], at(1 - 2 * side, 0))

    def edge_copy(to_right, block):
        dlat = 1 - block
        if to_right:
            return remote(edge_right, from_left.at[block], s_er.at[block], r_er.at[block], at(dlat, 1))
        return remote(edge_left, from_right.at[block], s_el.at[block], r_el.at[block], at(dlat, -1))

    sends = (has_dn, has_up)
    receives = (has_up, has_dn)

    pl.semaphore_wait(barrier, len(peers))
    fetched[0].wait()
    fetched[1].wait()

    def send_group(g):
        for side in range(2):
            @pl.when(sends[side])
            def _(side=side):
                main_copy(side, g).start()

    for side in range(2):
        @pl.when(sends[side])
        def _(side=side):
            aux_copy(side).start()
    early = groups // 2
    for g in range(early):
        send_group(g)

    def load(ref, f, g):
        return jnp.concatenate([ref[pl.ds(g * chunk + f * band + r, T, stride=per), :] for r in range(band)], 0)

    stack_lane = lax.broadcasted_iota(jnp.int32, (T * band, lanes), 1)
    stack_sub = lax.broadcasted_iota(jnp.int32, (T * band, lanes), 0)

    def seam_tiles(ref, f):
        tiles = roll(load(ref, f, groups - 1), slot * (groups - 1) + half_slot)
        for g in range(groups - 1):
            tiles = jnp.where(
                (stack_lane >= slot * g) & (stack_lane < slot * (g + 1)),
                roll(load(ref, f, g), slot * g + half_slot),
                tiles,
            )
        return tiles

    fetched[2].wait()
    fold = slot // edge
    own_seams = []
    tiles_per = band // fold
    in_slot = lax.rem(lane8, slot)
    for f in range(3):
        seams = seam_tiles(fac_ref, f)
        own_seams.append(seams)
        for t in range(tiles_per):
            right = left = None
            for q in range(fold):
                tile = seams[T * (t * fold + q) : T * (t * fold + q + 1)]
                to_right = roll(tile, edge * q - (half_slot - edge))
                to_left = roll(tile, edge * q - half_slot)
                keep = (in_slot >= edge * q) & (in_slot < edge * (q + 1))
                right = to_right if q == 0 else jnp.where(keep, to_right, right)
                left = to_left if q == 0 else jnp.where(keep, to_left, left)
            row = T * (f * tiles_per + t)
            edge_right[row : row + T, :] = right
            edge_left[row : row + T, :] = left
    aux_edge = None
    for f in range(4):
        tile = roll(aux[f * band : (f + 1) * band, :], 2 * edge * f + edge)
        aux_edge = tile if f == 0 else jnp.where(lane8 >= 2 * edge * f, tile, aux_edge)
    edge_rows = T * 3 * tiles_per
    edge_right[edge_rows:, :] = aux_edge
    edge_left[edge_rows:, :] = aux_edge

    for block in (1, 0, 2):
        def go(block=block):
            edge_copy(True, block).start()
            edge_copy(False, block).start()
        if block == 1:
            go()
        else:
            pl.when(sends[0] if block == 0 else sends[1])(go)
    for g in range(early, groups):
        send_group(g)

    for copy in fetched[3:]:
        copy.wait()
    cells = cells_ref[...]
    slots = cells.shape[1]
    live = lax.broadcasted_iota(jnp.int32, (1, slots), 1) < count_ref[...]
    weight = jnp.where(live, 1.0, 0.0) / err_ref[...]
    square = weight * weight
    obs_row = jnp.zeros_like(cells)
    for r in range(1, band):
        obs_row = obs_row + jnp.where(cells >= r * lanes, 1, 0)
    obs_col = cells - lanes * obs_row
    row_hot = lax.broadcasted_iota(jnp.int32, (band, slots), 0) == obs_row
    sums = jnp.concatenate(
        [jnp.where(row_hot, square, 0.0), jnp.where(row_hot, square * vals_ref[...], 0.0)], 0
    )
    col_hot = jnp.where(lax.broadcasted_iota(jnp.int32, (lanes, slots), 0) == obs_col, 1.0, 0.0)
    sums = lax.dot_general(
        jnp.concatenate(split(sums, 3), 0), col_hot.astype(jnp.bfloat16), NT, preferred_element_type=jnp.float32
    )
    sums = (sums[4 * band :] + sums[2 * band : 4 * band]) + sums[: 2 * band]
    cell_weight, cell_value = sums[:band], sums[band:]

    half = 0.5 * TIME_STEP
    up_gain = jnp.where(has_up, half, 0.0).astype(jnp.float32)
    down_gain = jnp.where(has_dn, half, 0.0).astype(jnp.float32)

    def spread(tile):
        return jnp.concatenate([jnp.broadcast_to(tile[r : r + 1], (T, lanes)) for r in range(band)], 0)

    for side in range(2):
        @pl.when(receives[side])
        def _(side=side):
            aux_copy(side).wait_recv()
    aux_blocks = (aux_up, aux, aux_dn)
    coef = jnp.concatenate([half * spread(b[3 * band :, :]) for b in aux_blocks], 0)

    blocks = (up_buf, fac_ref, dn_buf)

    def take_group(g):
        for side in range(2):
            @pl.when(receives[side])
            def _(side=side):
                main_copy(side, g).wait_recv()
        state = []
        for f in range(3):
            loaded = [load(b, f, g) for b in blocks]
            state.append(jnp.concatenate(loaded, 0))
            for side in range(2):
                spot = (side * 3 + f,)
                tiles = roll(loaded[2 * side], slot * g + half_slot)
                if g > 0:
                    tiles = jnp.where(stack_lane >= slot * g, tiles, seam_buf[spot])
                seam_buf[spot] = tiles
        state = evolve(*state, coef, up_gain, down_gain, band)
        for f in range(3):
            for r in range(band):
                fc[f * band + r, T * g : T * (g + 1), :] = state[f][T * r : T * (r + 1)]

    for g in range(early):
        take_group(g)

    edge_copy(True, 1).wait_recv()
    edge_copy(False, 1).wait_recv()
    for side in range(2):
        @pl.when(receives[side])
        def _(side=side):
            edge_copy(True, 2 * side).wait_recv()
            edge_copy(False, 2 * side).wait_recv()

    def aux_pair(b, f):
        own = aux_blocks[b][f * band : (f + 1) * band, :]
        left = from_left[b, edge_rows:, :]
        right = from_right[b, edge_rows:, :]
        strips = jnp.where(lane8 < half_slot, roll(left, half_slot - edge - 2 * edge * f), roll(own, half_slot))
        strips = jnp.where(
            lane8 < slot,
            strips,
            jnp.where(lane8 < slot + half_slot, roll(own, slot + half_slot), roll(right, slot + half_slot - edge - 2 * edge * f)),
        )
        return own, strips

    def mean_group(b, f):
        own, strips = aux_pair(b, f)
        return jnp.concatenate([jnp.where(sub8 == 0, own[r : r + 1], strips[r : r + 1]) for r in range(band)], 0)

    mean_state = [jnp.concatenate([mean_group(b, f) for b in range(3)], 0) for f in range(4)]
    mean_state = evolve(*mean_state[:3], half * mean_state[3], up_gain, down_gain, band)
    mean = []
    for f in range(3):
        strips = roll(mean_state[f], -1, 0)
        low = roll(strips, -half_slot)
        high = roll(strips, lanes - half_slot - slot)
        mean.append(jnp.where(stack_lane < edge, low, jnp.where(stack_lane >= lanes - edge, high, mean_state[f])))

    def repeat_slots(tile):
        tile = jnp.where(lane8 < slot, tile, 0.0)
        total = tile
        for g in range(1, groups):
            total = total + roll(tile, slot * g)
        return total

    strips_of = [aux_pair(b, 3)[1] for b in range(3)]
    coef_left = jnp.concatenate([half * spread(repeat_slots(s)) for s in strips_of], 0)
    coef_right = jnp.concatenate([half * spread(repeat_slots(roll(s, -slot))) for s in strips_of], 0)

    for g in range(early, groups):
        take_group(g)

    def unpack(ref, b, f, first):
        out = []
        for r in range(band):
            row = T * (f * tiles_per + r // fold)
            out.append(roll(ref[b, row : row + T, :], first - edge * (r % fold)))
        return jnp.concatenate(out, 0)

    low_half = lax.rem(stack_lane, slot) < half_slot
    left_state, right_state = [], []
    for f in range(3):
        lefts, rights = [], []
        for b in range(3):
            seams = own_seams[f] if b == 1 else seam_buf[(b // 2) * 3 + f]
            lefts.append(jnp.where(low_half, unpack(from_left, b, f, half_slot - edge), seams))
            rights.append(jnp.where(low_half, seams, unpack(from_right, b, f, half_slot)))
        left_state.append(jnp.concatenate(lefts, 0))
        right_state.append(jnp.concatenate(rights, 0))
    left_state = evolve(*left_state, coef_left, up_gain, down_gain, band)
    right_state = evolve(*right_state, coef_right, up_gain, down_gain, band)
    at_edge = (lane8 < edge) | (lane8 >= lanes - edge)

    def merge(f):
        seams = jnp.where(low_half, right_state[f], left_state[f])
        for g in range(groups):
            back = roll(seams, -(slot * g + half_slot))
            for r in range(band):
                spot = (f * band + r, slice(T * g, T * (g + 1)), slice(None))
                fc[spot] = jnp.where(at_edge, back[T * r : T * (r + 1)], fc[spot])

    merge(0)
    lhs, rhs = [], []
    for r in range(band):
        height = fc[r]
        w = cell_weight[r : r + 1]
        drive = cell_value[r : r + 1] - w * mean[0][T * r : T * r + 1]
        lhs.append(height)
        pad = jnp.zeros((lanes // 2 - rank - T, lanes), jnp.float32)
        rhs.append(jnp.concatenate([height * w, jnp.where(sub8 == 0, drive, 0.0), pad], 0))
    gram = lax.dot_general(
        jnp.concatenate(split(jnp.concatenate(lhs, 1), 2), 0),
        jnp.concatenate(split(jnp.concatenate(rhs, 1), 2), 0),
        NT, preferred_element_type=jnp.float32,
    )
    gram = gram[:rank] + gram[rank:]
    gram = gram + roll(gram, lanes // 2)
    hr = rank // 2
    wide = lax.broadcasted_iota(jnp.int32, (hr, lanes), 1)
    mine = jnp.where(wide < lanes // 2, gram[:hr], gram[hr:])

    p1[...] = mine
    def lat_copy(o):
        return remote(p1, ar1.at[o - 1], s1.at[o - 1], r1.at[o - 1], at(o, 0))
    def lon_copy(o):
        return remote(p2, ar2.at[o - 1], s2.at[o - 1], r2.at[o - 1], at(0, o))
    for o in range(1, n_lat):
        lat_copy(o).start()
    merge(1)
    merge(2)
    for f in range(3):
        for r in range(band):
            mean_out[f * band + r : f * band + r + 1, :] = mean[f][T * r : T * r + 1]
    for o in range(1, n_lat):
        lat_copy(o).wait_recv()
        mine = mine + ar1[o - 1]
    p2[...] = mine
    for o in range(1, n_lon):
        lon_copy(o).start()
    for o in range(1, n_lon):
        lon_copy(o).wait_recv()
        mine = mine + ar2[o - 1]

    gram_out[...] = mine

    for side in range(2):
        @pl.when(sends[side])
        def _(side=side):
            aux_copy(side).wait_send()
            for g in range(groups):
                main_copy(side, g).wait_send()
            edge_copy(True, 2 * side).wait_send()
            edge_copy(False, 2 * side).wait_send()
    edge_copy(True, 1).wait_send()
    edge_copy(False, 1).wait_send()
    for o in range(1, n_lat):
        lat_copy(o).wait_send()
    for o in range(1, n_lon):
        lon_copy(o).wait_send()


def transform(rank, fc, mean_ref, gram_ref, upd_hbm, out_hbm, upd, res, s_out):
    mine = gram_ref[...]
    lanes = mine.shape[1]
    band = fc.shape[0] // 3
    groups = rank // T
    sub8 = lax.broadcasted_iota(jnp.int32, (T, lanes), 0)
    both = jnp.concatenate([mine, roll(mine, lanes // 2)], 0)
    ri = lax.broadcasted_iota(jnp.int32, (rank, lanes), 0)
    li = lax.broadcasted_iota(jnp.int32, (rank, lanes), 1)
    eyes = jnp.where((li == ri) | (li == ri + lanes // 2), 1.0, 0.0)
    x = jnp.where(li < lanes // 2, both, 0.0) + eyes
    tiles = [x[T * i : T * (i + 1)] for i in range(groups)]
    for b in range(groups):
        cols = {
            (i, q): jnp.broadcast_to(tiles[i][:, T * b + q : T * b + q + 1], (T, lanes))
            for i in range(b, groups)
            for q in range(T)
        }
        for q in range(T):
            inv = 1.0 / cols[b, q][q : q + 1]
            row = tiles[b][q : q + 1]
            heads = [cols[b, p][q : q + 1] for p in range(q + 1, T)]
            for i in range(b, groups):
                if i == b and q == T - 1:
                    continue
                m = cols[i, q] * inv
                if i == b:
                    m = jnp.where(sub8 > q, m, 0.0)
                for p in range(q + 1, T):
                    cols[i, p] = cols[i, p] - m * heads[p - q - 1]
                tiles[i] = tiles[i] - m * row
    x = jnp.concatenate(tiles, 0)
    pivot = jnp.sum(jnp.where(li == ri, x, 0.0), 1, keepdims=True)
    x = x / jnp.sqrt(pivot)
    inverse = jnp.where(li < rank, roll(x, -(lanes // 2)), 0.0)
    z = x[:, rank : rank + 1]
    shift = jnp.sum(inverse * z, 0, keepdims=True)
    coefs = jnp.concatenate([inverse, jnp.where(sub8 == 0, shift, 0.0)], 0)
    high, low = (c.astype(jnp.float32) for c in split(coefs, 2))
    stacked = (high + roll(high, rank) + roll(low, 2 * rank))[:, : 3 * rank].astype(jnp.bfloat16)

    per = 3 * band
    for f in range(3):
        slab = jnp.concatenate([fc[f * band + r] for r in range(band)], 1)
        high, low = split(slab, 2)
        part = jnp.dot(stacked, jnp.concatenate([high, low, high], 0), preferred_element_type=jnp.float32)
        for r in range(band):
            col = part[:, lanes * r : lanes * (r + 1)]
            i = f * band + r
            for g in range(groups):
                res[pl.ds(g * T * per + i, T, stride=per), :] = col[T * g : T * (g + 1)]
            upd[i : i + 1, :] = mean_ref[i : i + 1, :] + col[rank : rank + 1]
    copies = [
        pltpu.make_async_copy(res, out_hbm, s_out.at[0]),
        pltpu.make_async_copy(upd, upd_hbm, s_out.at[1]),
    ]
    for copy in copies:
        copy.start()
    for copy in copies:
        copy.wait()


def in_hbm(x):
    return pltpu.with_memory_space_constraint(x, pltpu.HBM)


def per_device(n_lat, n_lon, background, factor, depth, cells, count, values, error):
    rank, fields, band, lanes = factor.shape
    groups = rank // T
    rows = rank * fields * band
    slots = cells.shape[0]
    assert band == T and 2 * STEPS <= band and rank % T == 0 and fields == 3
    edge_rows = T * (fields * band * groups * 2 * STEPS // lanes + 1)
    vmem = pl.BlockSpec(memory_space=pltpu.VMEM)
    f32 = functools.partial(pltpu.VMEM, dtype=jnp.float32)
    dma = pltpu.SemaphoreType.DMA
    anywhere = pl.BlockSpec(memory_space=pl.ANY)
    forecast, mean, gram = pl.pallas_call(
        functools.partial(kernel, n_lat, n_lon, rank),
        out_shape=(
            jax.ShapeDtypeStruct((fields * band, rank, lanes), jnp.float32),
            jax.ShapeDtypeStruct((fields * band, lanes), jnp.float32),
            jax.ShapeDtypeStruct((rank // 2, lanes), jnp.float32),
        ),
        in_specs=[pl.BlockSpec(memory_space=pltpu.HBM)] * 7,
        out_specs=(vmem, vmem, vmem),
        scratch_shapes=[
            f32((rows, lanes)), pltpu.VMEM((1, slots), jnp.int32), pltpu.VMEM((1, 1), jnp.int32),
            f32((1, slots)), f32((1, slots)), dma((7,)),
            f32((rows, lanes)), f32((rows, lanes)),
            f32((4 * band, lanes)), f32((4 * band, lanes)), f32((4 * band, lanes)),
            f32((edge_rows, lanes)), f32((edge_rows, lanes)),
            f32((3, edge_rows, lanes)), f32((3, edge_rows, lanes)),
            f32((2 * fields, T * band, lanes)), f32((rank // 2, lanes)), f32((rank // 2, lanes)),
            f32((n_lat - 1, rank // 2, lanes)), f32((n_lon - 1, rank // 2, lanes)),
            dma((2, groups)), dma((2, groups)), dma((2,)), dma((2,)),
            dma((3,)), dma((3,)), dma((3,)), dma((3,)),
            dma((n_lat - 1,)), dma((n_lat - 1,)), dma((n_lon - 1,)), dma((n_lon - 1,)),
        ],
        compiler_params=pltpu.CompilerParams(
            collective_id=0, has_side_effects=True, vmem_limit_bytes=32 * 1024 * 1024
        ),
    )(
        in_hbm(background.reshape(fields * band, lanes)), in_hbm(factor.reshape(rows, lanes)), in_hbm(depth),
        in_hbm(cells.reshape(1, slots)), count.reshape(1, 1), in_hbm(values.reshape(1, slots)), in_hbm(error.reshape(1, slots)),
    )
    updated, analysis = pl.pallas_call(
        functools.partial(transform, rank),
        out_shape=(
            jax.ShapeDtypeStruct((fields * band, lanes), jnp.float32),
            jax.ShapeDtypeStruct((rows, lanes), jnp.float32),
        ),
        in_specs=[vmem] * 3,
        out_specs=(anywhere, anywhere),
        scratch_shapes=[f32((fields * band, lanes)), f32((rows, lanes)), dma((2,))],
        compiler_params=pltpu.CompilerParams(vmem_limit_bytes=16 * 1024 * 1024),
    )(forecast, mean, gram)
    return updated.reshape(background.shape), analysis.reshape(factor.shape)


def solution(mesh):
    return jax.shard_map(
        functools.partial(per_device, mesh.shape["lat"], mesh.shape["lon"]),
        mesh=mesh,
        in_specs=(
            P(None, "lat", "lon"),
            P(None, None, "lat", "lon"),
            P("lat", "lon"),
            P(("lat", "lon")),
            P(("lat", "lon")),
            P(("lat", "lon")),
            P(("lat", "lon")),
        ),
        out_specs=(P(None, "lat", "lon"), P(None, None, "lat", "lon")),
        check_vma=False,
    )
```

```python
import functools

import jax
import jax.numpy as jnp
from jax import lax
from jax.experimental import pallas as pl
from jax.experimental.pallas import tpu as pltpu
from jax.sharding import PartitionSpec as P

STEPS = 4
TIME_STEP = 0.9
ROTATION = 0.25
MESH = pl.DeviceIdType.MESH
T = 8
NT = (((1,), (1,)), ((), ()))


def roll(x, shift, axis=1):
    shift = shift % x.shape[axis]
    return x if shift == 0 else pltpu.roll(x, shift, axis)


def split(x, terms):
    parts = []
    for _ in range(terms):
        part = x.astype(jnp.bfloat16)
        parts.append(part)
        x = x - part.astype(jnp.float32)
    return parts


def evolve(h, e, n, coef, up_gain, down_gain, band):
    half = 0.5 * TIME_STEP
    for step in range(STEPS):
        w = 2 * (STEPS - step)
        last = coef.shape[0] - T * (band - w + 1)
        mid = e[T:-T]
        div = (roll(mid, -1) - roll(mid, 1)) + (n[2 * T :] - n[: -2 * T])
        hn = h[T:-T] - coef[T * (band - w + 1) : last] * div
        inner = hn[T:-T]
        shape = (T * (w - 2), h.shape[1])
        parts = [jnp.full((T * band, h.shape[1]), half, jnp.float32)]
        if w > 2:
            parts = [jnp.full(shape, up_gain)] + parts + [jnp.full(shape, down_gain)]
        gain = jnp.concatenate(parts, 0) if w > 2 else parts[0]
        e0, n0 = e[2 * T : -2 * T], n[2 * T : -2 * T]
        e = e0 - half * (roll(inner, -1) - roll(inner, 1)) + ROTATION * n0
        n = n0 - gain * (hn[2 * T :] - hn[: -2 * T]) - ROTATION * e0
        h = inner
    return h, e, n


def kernel(
    n_lat, n_lon, rank,
    mean_hbm, fac_hbm, depth_hbm, cells_hbm, count_hbm, vals_hbm, err_hbm,
    fc, mean_out, gram_out,
    fac_ref, cells_ref, count_ref, vals_ref, err_ref, s_in,
    up_buf, dn_buf, aux, aux_up, aux_dn, edge_right, edge_left, from_left, from_right,
    seam_buf, own_seams, coef_buf, strip_state, strip_out, p1, p2, ar1, ar2,
    s_main, r_main, s_aux, r_aux, s_el, r_el, s_er, r_er, s1, r1, s2, r2,
):
    lat, lon = lax.axis_index("lat"), lax.axis_index("lon")
    band, lanes = depth_hbm.shape
    groups = rank // T
    slot = lanes // groups
    half_slot = slot // 2
    edge = 2 * STEPS
    per = 3 * band
    chunk = T * per
    lane8 = lax.broadcasted_iota(jnp.int32, (T, lanes), 1)
    sub8 = lax.broadcasted_iota(jnp.int32, (T, lanes), 0)

    def at(dlat, dlon):
        return (lax.rem(lat + dlat + n_lat, n_lat), lax.rem(lon + dlon + n_lon, n_lon))

    diagonals = [(a, b) for a in (-1, 1) for b in (-1, 1)]
    peers = [(a, 0) for a in range(1, n_lat)] + [(0, b) for b in range(1, n_lon)] + diagonals
    barrier = pltpu.get_barrier_semaphore()
    for a, b in peers:
        pl.semaphore_signal(barrier, inc=1, device_id=at(a, b), device_id_type=MESH)

    has_up, has_dn = lat > 0, lat < n_lat - 1
    fetched = [
        pltpu.make_async_copy(src, dst, s_in.at[i])
        for i, (src, dst) in enumerate((
            (mean_hbm, aux.at[pl.ds(0, 3 * band)]),
            (depth_hbm, aux.at[pl.ds(3 * band, band)]),
            (fac_hbm, fac_ref),
            (cells_hbm, cells_ref),
            (count_hbm, count_ref),
            (vals_hbm, vals_ref),
            (err_hbm, err_ref),
        ))
    ]
    for copy in fetched:
        copy.start()

    @pl.when(jnp.logical_not(has_up))
    def _():
        up_buf[...] = jnp.zeros_like(up_buf)
        aux_up[...] = jnp.zeros_like(aux_up)
        from_left[0] = jnp.zeros_like(from_left[0])
        from_right[0] = jnp.zeros_like(from_right[0])

    @pl.when(jnp.logical_not(has_dn))
    def _():
        dn_buf[...] = jnp.zeros_like(dn_buf)
        aux_dn[...] = jnp.zeros_like(aux_dn)
        from_left[2] = jnp.zeros_like(from_left[2])
        from_right[2] = jnp.zeros_like(from_right[2])

    def remote(src, dst, ssem, rsem, where):
        return pltpu.make_async_remote_copy(
            src_ref=src, dst_ref=dst, send_sem=ssem, recv_sem=rsem, device_id=where, device_id_type=MESH
        )

    def main_copy(side, g):
        rows = pl.ds(g * chunk, chunk)
        dst = (up_buf, dn_buf)[side]
        return remote(fac_hbm.at[rows], dst.at[rows], s_main.at[side, g], r_main.at[side, g], at(1 - 2 * side, 0))

    def aux_copy(side):
        dst = (aux_up, aux_dn)[side]
        return remote(aux, dst, s_aux.at[side], r_aux.at[side], at(1 - 2 * side, 0))

    def edge_copy(to_right, block):
        dlat = 1 - block
        if to_right:
            return remote(edge_right, from_left.at[block], s_er.at[block], r_er.at[block], at(dlat, 1))
        return remote(edge_left, from_right.at[block], s_el.at[block], r_el.at[block], at(dlat, -1))

    sends = (has_dn, has_up)
    receives = (has_up, has_dn)

    pl.semaphore_wait(barrier, len(peers))
    fetched[0].wait()
    fetched[1].wait()

    def send_group(g):
        for side in range(2):
            @pl.when(sends[side])
            def _(side=side):
                main_copy(side, g).start()

    for side in range(2):
        @pl.when(sends[side])
        def _(side=side):
            aux_copy(side).start()
    early = groups // 2
    for g in range(early):
        send_group(g)

    def load(ref, f, g):
        return jnp.concatenate([ref[pl.ds(g * chunk + f * band + r, T, stride=per), :] for r in range(band)], 0)

    stack_lane = lax.broadcasted_iota(jnp.int32, (T * band, lanes), 1)
    stack_sub = lax.broadcasted_iota(jnp.int32, (T * band, lanes), 0)

    def seam_tiles(ref, f):
        tiles = roll(load(ref, f, groups - 1), slot * (groups - 1) + half_slot)
        for g in range(groups - 1):
            tiles = jnp.where(
                (stack_lane >= slot * g) & (stack_lane < slot * (g + 1)),
                roll(load(ref, f, g), slot * g + half_slot),
                tiles,
            )
        return tiles

    fetched[2].wait()
    fold = slot // edge
    tiles_per = band // fold
    in_slot = lax.rem(lane8, slot)

    def pack(f, carry):
        seams = seam_tiles(fac_ref, f)
        own_seams[f] = seams
        for t in range(tiles_per):
            right = left = None
            for q in range(fold):
                tile = seams[T * (t * fold + q) : T * (t * fold + q + 1)]
                to_right = roll(tile, edge * q - (half_slot - edge))
                to_left = roll(tile, edge * q - half_slot)
                keep = (in_slot >= edge * q) & (in_slot < edge * (q + 1))
                right = to_right if q == 0 else jnp.where(keep, to_right, right)
                left = to_left if q == 0 else jnp.where(keep, to_left, left)
            row = pl.ds(pl.multiple_of(T * (f * tiles_per + t), T), T)
            edge_right[row, :] = right
            edge_left[row, :] = left
        return carry

    lax.fori_loop(0, 3, pack, 0)
    aux_edge = None
    for f in range(4):
        tile = roll(aux[f * band : (f + 1) * band, :], 2 * edge * f + edge)
        aux_edge = tile if f == 0 else jnp.where(lane8 >= 2 * edge * f, tile, aux_edge)
    edge_rows = T * 3 * tiles_per
    edge_right[edge_rows:, :] = aux_edge
    edge_left[edge_rows:, :] = aux_edge

    for block in (1, 0, 2):
        def go(block=block):
            edge_copy(True, block).start()
            edge_copy(False, block).start()
        if block == 1:
            go()
        else:
            pl.when(sends[0] if block == 0 else sends[1])(go)
    for g in range(early, groups):
        send_group(g)

    for copy in fetched[3:]:
        copy.wait()
    cells = cells_ref[...]
    slots = cells.shape[1]
    live = lax.broadcasted_iota(jnp.int32, (1, slots), 1) < count_ref[...]
    weight = jnp.where(live, 1.0, 0.0) / err_ref[...]
    square = weight * weight
    obs_row = jnp.zeros_like(cells)
    for r in range(1, band):
        obs_row = obs_row + jnp.where(cells >= r * lanes, 1, 0)
    obs_col = cells - lanes * obs_row
    row_hot = lax.broadcasted_iota(jnp.int32, (band, slots), 0) == obs_row
    sums = jnp.concatenate(
        [jnp.where(row_hot, square, 0.0), jnp.where(row_hot, square * vals_ref[...], 0.0)], 0
    )
    col_hot = jnp.where(lax.broadcasted_iota(jnp.int32, (lanes, slots), 0) == obs_col, 1.0, 0.0)
    sums = lax.dot_general(
        jnp.concatenate(split(sums, 3), 0), col_hot.astype(jnp.bfloat16), NT, preferred_element_type=jnp.float32
    )
    sums = (sums[4 * band :] + sums[2 * band : 4 * band]) + sums[: 2 * band]
    cell_weight, cell_value = sums[:band], sums[band:]

    half = 0.5 * TIME_STEP
    up_gain = jnp.where(has_up, half, 0.0).astype(jnp.float32)
    down_gain = jnp.where(has_dn, half, 0.0).astype(jnp.float32)

    def spread(tile):
        return jnp.concatenate([jnp.broadcast_to(tile[r : r + 1], (T, lanes)) for r in range(band)], 0)

    for side in range(2):
        @pl.when(receives[side])
        def _(side=side):
            aux_copy(side).wait_recv()
    aux_blocks = (aux_up, aux, aux_dn)
    for b in range(3):
        coef_buf[3, T * band * b : T * band * (b + 1), :] = half * spread(aux_blocks[b][3 * band :, :])
    seam_buf[...] = jnp.zeros_like(seam_buf)

    blocks = (up_buf, fac_ref, dn_buf)

    def take_group(g, carry):
        for side in range(2):
            @pl.when(receives[side])
            def _(side=side):
                main_copy(side, g).wait_recv()
        state = []
        for f in range(3):
            loaded = [load(b, f, g) for b in blocks]
            state.append(jnp.concatenate(loaded, 0))
            for side in range(2):
                spot = (side * 3 + f,)
                tiles = pltpu.roll(loaded[2 * side], slot * g + half_slot, 1)
                seam_buf[spot] = jnp.where(stack_lane >= slot * g, tiles, seam_buf[spot])
        state = evolve(*state, coef_buf[3], up_gain, down_gain, band)
        spot = pl.ds(pl.multiple_of(T * g, T), T)
        for f in range(3):
            for r in range(band):
                fc[f * band + r, spot, :] = state[f][T * r : T * (r + 1)]
        return carry

    lax.fori_loop(0, groups, take_group, 0)

    edge_copy(True, 1).wait_recv()
    edge_copy(False, 1).wait_recv()
    for side in range(2):
        @pl.when(receives[side])
        def _(side=side):
            edge_copy(True, 2 * side).wait_recv()
            edge_copy(False, 2 * side).wait_recv()

    def aux_pair(b, f):
        own = aux_blocks[b][f * band : (f + 1) * band, :]
        left = from_left[b, edge_rows:, :]
        right = from_right[b, edge_rows:, :]
        strips = jnp.where(lane8 < half_slot, roll(left, half_slot - edge - 2 * edge * f), roll(own, half_slot))
        strips = jnp.where(
            lane8 < slot,
            strips,
            jnp.where(lane8 < slot + half_slot, roll(own, slot + half_slot), roll(right, slot + half_slot - edge - 2 * edge * f)),
        )
        return own, strips

    def mean_group(b, f):
        own, strips = aux_pair(b, f)
        return jnp.concatenate([jnp.where(sub8 == 0, own[r : r + 1], strips[r : r + 1]) for r in range(band)], 0)

    def repeat_slots(tile):
        tile = jnp.where(lane8 < slot, tile, 0.0)
        total = tile
        for g in range(1, groups):
            total = total + roll(tile, slot * g)
        return total

    strips_of = [aux_pair(b, 3)[1] for b in range(3)]
    for b in range(3):
        rows = slice(T * band * b, T * band * (b + 1))
        coef_buf[0, rows, :] = half * spread(repeat_slots(strips_of[b]))
        coef_buf[1, rows, :] = half * spread(repeat_slots(roll(strips_of[b], -slot)))
        coef_buf[2, rows, :] = half * mean_group(b, 3)
        for f in range(3):
            strip_state[2, f, rows, :] = mean_group(b, f)

    def unpack(ref, b, f, first):
        out = []
        for r in range(band):
            row = pl.ds(pl.multiple_of(T * (f * tiles_per + r // fold), T), T)
            out.append(roll(ref[b, row, :], first - edge * (r % fold)))
        return jnp.concatenate(out, 0)

    low_half = lax.rem(stack_lane, slot) < half_slot

    def join(f, carry):
        for b in range(3):
            rows = slice(T * band * b, T * band * (b + 1))
            seams = own_seams[f] if b == 1 else seam_buf[(b // 2) * 3 + f]
            strip_state[0, f, rows, :] = jnp.where(low_half, unpack(from_left, b, f, half_slot - edge), seams)
            strip_state[1, f, rows, :] = jnp.where(low_half, seams, unpack(from_right, b, f, half_slot))
        return carry

    lax.fori_loop(0, 3, join, 0)

    def take_strips(u, carry):
        state = evolve(*(strip_state[u, f] for f in range(3)), coef_buf[u], up_gain, down_gain, band)
        for f in range(3):
            strip_out[u, f] = state[f]
        return carry

    lax.fori_loop(0, 3, take_strips, 0)
    mean = []
    for f in range(3):
        whole = strip_out[2, f]
        strips = roll(whole, -1, 0)
        low = roll(strips, -half_slot)
        high = roll(strips, lanes - half_slot - slot)
        mean.append(jnp.where(stack_lane < edge, low, jnp.where(stack_lane >= lanes - edge, high, whole)))
    at_edge = (lane8 < edge) | (lane8 >= lanes - edge)

    def merge(f):
        seams = jnp.where(low_half, strip_out[1, f], strip_out[0, f])

        def one(g, carry):
            back = pltpu.roll(seams, lanes - (slot * g + half_slot), 1)
            for r in range(band):
                spot = (f * band + r, pl.ds(pl.multiple_of(T * g, T), T), slice(None))
                fc[spot] = jnp.where(at_edge, back[T * r : T * (r + 1)], fc[spot])
            return carry

        lax.fori_loop(0, groups, one, 0)

    merge(0)
    lhs, rhs = [], []
    for r in range(band):
        height = fc[r]
        w = cell_weight[r : r + 1]
        drive = cell_value[r : r + 1] - w * mean[0][T * r : T * r + 1]
        lhs.append(height)
        pad = jnp.zeros((lanes // 2 - rank - T, lanes), jnp.float32)
        rhs.append(jnp.concatenate([height * w, jnp.where(sub8 == 0, drive, 0.0), pad], 0))
    gram = lax.dot_general(
        jnp.concatenate(split(jnp.concatenate(lhs, 1), 2), 0),
        jnp.concatenate(split(jnp.concatenate(rhs, 1), 2), 0),
        NT, preferred_element_type=jnp.float32,
    )
    gram = gram[:rank] + gram[rank:]
    gram = gram + roll(gram, lanes // 2)
    hr = rank // 2
    wide = lax.broadcasted_iota(jnp.int32, (hr, lanes), 1)
    mine = jnp.where(wide < lanes // 2, gram[:hr], gram[hr:])

    p1[...] = mine
    def lat_copy(o):
        return remote(p1, ar1.at[o - 1], s1.at[o - 1], r1.at[o - 1], at(o, 0))
    def lon_copy(o):
        return remote(p2, ar2.at[o - 1], s2.at[o - 1], r2.at[o - 1], at(0, o))
    for o in range(1, n_lat):
        lat_copy(o).start()
    merge(1)
    merge(2)
    for f in range(3):
        for r in range(band):
            mean_out[f * band + r : f * band + r + 1, :] = mean[f][T * r : T * r + 1]
    for o in range(1, n_lat):
        lat_copy(o).wait_recv()
        mine = mine + ar1[o - 1]
    p2[...] = mine
    for o in range(1, n_lon):
        lon_copy(o).start()
    for o in range(1, n_lon):
        lon_copy(o).wait_recv()
        mine = mine + ar2[o - 1]

    gram_out[...] = mine

    for side in range(2):
        @pl.when(sends[side])
        def _(side=side):
            aux_copy(side).wait_send()
            for g in range(groups):
                main_copy(side, g).wait_send()
            edge_copy(True, 2 * side).wait_send()
            edge_copy(False, 2 * side).wait_send()
    edge_copy(True, 1).wait_send()
    edge_copy(False, 1).wait_send()
    for o in range(1, n_lat):
        lat_copy(o).wait_send()
    for o in range(1, n_lon):
        lon_copy(o).wait_send()


def transform(rank, fc, mean_ref, gram_ref, upd_hbm, out_hbm, upd, res, s_out):
    mine = gram_ref[...]
    lanes = mine.shape[1]
    band = fc.shape[0] // 3
    groups = rank // T
    sub8 = lax.broadcasted_iota(jnp.int32, (T, lanes), 0)
    both = jnp.concatenate([mine, roll(mine, lanes // 2)], 0)
    ri = lax.broadcasted_iota(jnp.int32, (rank, lanes), 0)
    li = lax.broadcasted_iota(jnp.int32, (rank, lanes), 1)
    eyes = jnp.where((li == ri) | (li == ri + lanes // 2), 1.0, 0.0)
    x = jnp.where(li < lanes // 2, both, 0.0) + eyes
    tiles = [x[T * i : T * (i + 1)] for i in range(groups)]
    for b in range(groups):
        cols = {
            (i, q): jnp.broadcast_to(tiles[i][:, T * b + q : T * b + q + 1], (T, lanes))
            for i in range(b, groups)
            for q in range(T)
        }
        for q in range(T):
            inv = 1.0 / cols[b, q][q : q + 1]
            row = tiles[b][q : q + 1]
            heads = [cols[b, p][q : q + 1] for p in range(q + 1, T)]
            for i in range(b, groups):
                if i == b and q == T - 1:
                    continue
                m = cols[i, q] * inv
                if i == b:
                    m = jnp.where(sub8 > q, m, 0.0)
                for p in range(q + 1, T):
                    cols[i, p] = cols[i, p] - m * heads[p - q - 1]
                tiles[i] = tiles[i] - m * row
    x = jnp.concatenate(tiles, 0)
    pivot = jnp.sum(jnp.where(li == ri, x, 0.0), 1, keepdims=True)
    x = x / jnp.sqrt(pivot)
    inverse = jnp.where(li < rank, roll(x, -(lanes // 2)), 0.0)
    z = x[:, rank : rank + 1]
    shift = jnp.sum(inverse * z, 0, keepdims=True)
    coefs = jnp.concatenate([inverse, jnp.where(sub8 == 0, shift, 0.0)], 0)
    high, low = (c.astype(jnp.float32) for c in split(coefs, 2))
    stacked = (high + roll(high, rank) + roll(low, 2 * rank))[:, : 3 * rank].astype(jnp.bfloat16)

    per = 3 * band
    for f in range(3):
        slab = jnp.concatenate([fc[f * band + r] for r in range(band)], 1)
        high, low = split(slab, 2)
        part = jnp.dot(stacked, jnp.concatenate([high, low, high], 0), preferred_element_type=jnp.float32)
        for r in range(band):
            col = part[:, lanes * r : lanes * (r + 1)]
            i = f * band + r
            for g in range(groups):
                res[pl.ds(g * T * per + i, T, stride=per), :] = col[T * g : T * (g + 1)]
            upd[i : i + 1, :] = mean_ref[i : i + 1, :] + col[rank : rank + 1]
    copies = [
        pltpu.make_async_copy(res, out_hbm, s_out.at[0]),
        pltpu.make_async_copy(upd, upd_hbm, s_out.at[1]),
    ]
    for copy in copies:
        copy.start()
    for copy in copies:
        copy.wait()


def in_hbm(x):
    return pltpu.with_memory_space_constraint(x, pltpu.HBM)


def per_device(n_lat, n_lon, background, factor, depth, cells, count, values, error):
    rank, fields, band, lanes = factor.shape
    groups = rank // T
    rows = rank * fields * band
    slots = cells.shape[0]
    assert band == T and 2 * STEPS <= band and rank % T == 0 and fields == 3
    edge_rows = T * (fields * band * groups * 2 * STEPS // lanes + 1)
    vmem = pl.BlockSpec(memory_space=pltpu.VMEM)
    f32 = functools.partial(pltpu.VMEM, dtype=jnp.float32)
    dma = pltpu.SemaphoreType.DMA
    anywhere = pl.BlockSpec(memory_space=pl.ANY)
    forecast, mean, gram = pl.pallas_call(
        functools.partial(kernel, n_lat, n_lon, rank),
        out_shape=(
            jax.ShapeDtypeStruct((fields * band, rank, lanes), jnp.float32),
            jax.ShapeDtypeStruct((fields * band, lanes), jnp.float32),
            jax.ShapeDtypeStruct((rank // 2, lanes), jnp.float32),
        ),
        in_specs=[pl.BlockSpec(memory_space=pltpu.HBM)] * 7,
        out_specs=(vmem, vmem, vmem),
        scratch_shapes=[
            f32((rows, lanes)), pltpu.VMEM((1, slots), jnp.int32), pltpu.VMEM((1, 1), jnp.int32),
            f32((1, slots)), f32((1, slots)), dma((7,)),
            f32((rows, lanes)), f32((rows, lanes)),
            f32((4 * band, lanes)), f32((4 * band, lanes)), f32((4 * band, lanes)),
            f32((edge_rows, lanes)), f32((edge_rows, lanes)),
            f32((3, edge_rows, lanes)), f32((3, edge_rows, lanes)),
            f32((2 * fields, T * band, lanes)), f32((fields, T * band, lanes)), f32((4, 3 * T * band, lanes)),
            f32((3, fields, 3 * T * band, lanes)), f32((3, fields, T * band, lanes)), f32((rank // 2, lanes)), f32((rank // 2, lanes)),
            f32((n_lat - 1, rank // 2, lanes)), f32((n_lon - 1, rank // 2, lanes)),
            dma((2, groups)), dma((2, groups)), dma((2,)), dma((2,)),
            dma((3,)), dma((3,)), dma((3,)), dma((3,)),
            dma((n_lat - 1,)), dma((n_lat - 1,)), dma((n_lon - 1,)), dma((n_lon - 1,)),
        ],
        compiler_params=pltpu.CompilerParams(
            collective_id=0, has_side_effects=True, vmem_limit_bytes=32 * 1024 * 1024
        ),
    )(
        in_hbm(background.reshape(fields * band, lanes)), in_hbm(factor.reshape(rows, lanes)), in_hbm(depth),
        in_hbm(cells.reshape(1, slots)), count.reshape(1, 1), in_hbm(values.reshape(1, slots)), in_hbm(error.reshape(1, slots)),
    )
    updated, analysis = pl.pallas_call(
        functools.partial(transform, rank),
        out_shape=(
            jax.ShapeDtypeStruct((fields * band, lanes), jnp.float32),
            jax.ShapeDtypeStruct((rows, lanes), jnp.float32),
        ),
        in_specs=[vmem] * 3,
        out_specs=(anywhere, anywhere),
        scratch_shapes=[f32((fields * band, lanes)), f32((rows, lanes)), dma((2,))],
        compiler_params=pltpu.CompilerParams(vmem_limit_bytes=16 * 1024 * 1024),
    )(forecast, mean, gram)
    return updated.reshape(background.shape), analysis.reshape(factor.shape)


def solution(mesh):
    return jax.shard_map(
        functools.partial(per_device, mesh.shape["lat"], mesh.shape["lon"]),
        mesh=mesh,
        in_specs=(
            P(None, "lat", "lon"),
            P(None, None, "lat", "lon"),
            P("lat", "lon"),
            P(("lat", "lon")),
            P(("lat", "lon")),
            P(("lat", "lon")),
            P(("lat", "lon")),
        ),
        out_specs=(P(None, "lat", "lon"), P(None, None, "lat", "lon")),
        check_vma=False,
    )
```

```python
import functools

import jax
import jax.numpy as jnp
from jax import lax
from jax.experimental import pallas as pl
from jax.experimental.pallas import tpu as pltpu
from jax.sharding import PartitionSpec as P

STEPS = 4
TIME_STEP = 0.9
ROTATION = 0.25
MESH = pl.DeviceIdType.MESH
T = 8
NT = (((1,), (1,)), ((), ()))


def roll(x, shift, axis=1):
    shift = shift % x.shape[axis]
    return x if shift == 0 else pltpu.roll(x, shift, axis)


def split(x, terms):
    parts = []
    for _ in range(terms):
        part = x.astype(jnp.bfloat16)
        parts.append(part)
        x = x - part.astype(jnp.float32)
    return parts


def evolve(h, e, n, coef, up_gain, down_gain, band):
    half = 0.5 * TIME_STEP
    for step in range(STEPS):
        w = 2 * (STEPS - step)
        last = coef.shape[0] - T * (band - w + 1)
        mid = e[T:-T]
        div = (roll(mid, -1) - roll(mid, 1)) + (n[2 * T :] - n[: -2 * T])
        hn = h[T:-T] - coef[T * (band - w + 1) : last] * div
        inner = hn[T:-T]
        shape = (T * (w - 2), h.shape[1])
        parts = [jnp.full((T * band, h.shape[1]), half, jnp.float32)]
        if w > 2:
            parts = [jnp.full(shape, up_gain)] + parts + [jnp.full(shape, down_gain)]
        gain = jnp.concatenate(parts, 0) if w > 2 else parts[0]
        e0, n0 = e[2 * T : -2 * T], n[2 * T : -2 * T]
        e = e0 - half * (roll(inner, -1) - roll(inner, 1)) + ROTATION * n0
        n = n0 - gain * (hn[2 * T :] - hn[: -2 * T]) - ROTATION * e0
        h = inner
    return h, e, n


def kernel(
    n_lat, n_lon, rank,
    mean_hbm, fac_hbm, depth_hbm, cells_hbm, count_hbm, vals_hbm, err_hbm,
    fc, mean_out, gram_out,
    fac_ref, cells_ref, count_ref, vals_ref, err_ref, s_in,
    up_buf, dn_buf, aux, aux_up, aux_dn, edge_right, edge_left, from_left, from_right,
    seam_buf,
    s_main, r_main, s_aux, r_aux, s_el, r_el, s_er, r_er,
):
    lat, lon = lax.axis_index("lat"), lax.axis_index("lon")
    band, lanes = depth_hbm.shape
    groups = rank // T
    slot = lanes // groups
    half_slot = slot // 2
    edge = 2 * STEPS
    per = 3 * band
    chunk = T * per
    lane8 = lax.broadcasted_iota(jnp.int32, (T, lanes), 1)
    sub8 = lax.broadcasted_iota(jnp.int32, (T, lanes), 0)

    def at(dlat, dlon):
        return (lax.rem(lat + dlat + n_lat, n_lat), lax.rem(lon + dlon + n_lon, n_lon))

    diagonals = [(a, b) for a in (-1, 1) for b in (-1, 1)]
    peers = [(-1, 0), (1, 0), (0, -1), (0, 1)] + diagonals
    barrier = pltpu.get_barrier_semaphore()
    for a, b in peers:
        pl.semaphore_signal(barrier, inc=1, device_id=at(a, b), device_id_type=MESH)

    has_up, has_dn = lat > 0, lat < n_lat - 1
    fetched = [
        pltpu.make_async_copy(src, dst, s_in.at[i])
        for i, (src, dst) in enumerate((
            (mean_hbm, aux.at[pl.ds(0, 3 * band)]),
            (depth_hbm, aux.at[pl.ds(3 * band, band)]),
            (fac_hbm, fac_ref),
            (cells_hbm, cells_ref),
            (count_hbm, count_ref),
            (vals_hbm, vals_ref),
            (err_hbm, err_ref),
        ))
    ]
    for copy in fetched:
        copy.start()

    @pl.when(jnp.logical_not(has_up))
    def _():
        up_buf[...] = jnp.zeros_like(up_buf)
        aux_up[...] = jnp.zeros_like(aux_up)
        from_left[0] = jnp.zeros_like(from_left[0])
        from_right[0] = jnp.zeros_like(from_right[0])

    @pl.when(jnp.logical_not(has_dn))
    def _():
        dn_buf[...] = jnp.zeros_like(dn_buf)
        aux_dn[...] = jnp.zeros_like(aux_dn)
        from_left[2] = jnp.zeros_like(from_left[2])
        from_right[2] = jnp.zeros_like(from_right[2])

    def remote(src, dst, ssem, rsem, where):
        return pltpu.make_async_remote_copy(
            src_ref=src, dst_ref=dst, send_sem=ssem, recv_sem=rsem, device_id=where, device_id_type=MESH
        )

    def main_copy(side, g):
        rows = pl.ds(g * chunk, chunk)
        dst = (up_buf, dn_buf)[side]
        return remote(fac_hbm.at[rows], dst.at[rows], s_main.at[side, g], r_main.at[side, g], at(1 - 2 * side, 0))

    def aux_copy(side):
        dst = (aux_up, aux_dn)[side]
        return remote(aux, dst, s_aux.at[side], r_aux.at[side], at(1 - 2 * side, 0))

    def edge_copy(to_right, block):
        dlat = 1 - block
        if to_right:
            return remote(edge_right, from_left.at[block], s_er.at[block], r_er.at[block], at(dlat, 1))
        return remote(edge_left, from_right.at[block], s_el.at[block], r_el.at[block], at(dlat, -1))

    sends = (has_dn, has_up)
    receives = (has_up, has_dn)

    pl.semaphore_wait(barrier, len(peers))
    fetched[0].wait()
    fetched[1].wait()

    def send_group(g):
        for side in range(2):
            @pl.when(sends[side])
            def _(side=side):
                main_copy(side, g).start()

    for side in range(2):
        @pl.when(sends[side])
        def _(side=side):
            aux_copy(side).start()
    early = groups // 2
    for g in range(early):
        send_group(g)

    def load(ref, f, g):
        return jnp.concatenate([ref[pl.ds(g * chunk + f * band + r, T, stride=per), :] for r in range(band)], 0)

    stack_lane = lax.broadcasted_iota(jnp.int32, (T * band, lanes), 1)
    stack_sub = lax.broadcasted_iota(jnp.int32, (T * band, lanes), 0)

    def seam_tiles(ref, f):
        tiles = roll(load(ref, f, groups - 1), slot * (groups - 1) + half_slot)
        for g in range(groups - 1):
            tiles = jnp.where(
                (stack_lane >= slot * g) & (stack_lane < slot * (g + 1)),
                roll(load(ref, f, g), slot * g + half_slot),
                tiles,
            )
        return tiles

    fetched[2].wait()
    fold = slot // edge
    own_seams = []
    tiles_per = band // fold
    in_slot = lax.rem(lane8, slot)
    for f in range(3):
        seams = seam_tiles(fac_ref, f)
        own_seams.append(seams)
        for t in range(tiles_per):
            right = left = None
            for q in range(fold):
                tile = seams[T * (t * fold + q) : T * (t * fold + q + 1)]
                to_right = roll(tile, edge * q - (half_slot - edge))
                to_left = roll(tile, edge * q - half_slot)
                keep = (in_slot >= edge * q) & (in_slot < edge * (q + 1))
                right = to_right if q == 0 else jnp.where(keep, to_right, right)
                left = to_left if q == 0 else jnp.where(keep, to_left, left)
            row = T * (f * tiles_per + t)
            edge_right[row : row + T, :] = right
            edge_left[row : row + T, :] = left
    aux_edge = None
    for f in range(4):
        tile = roll(aux[f * band : (f + 1) * band, :], 2 * edge * f + edge)
        aux_edge = tile if f == 0 else jnp.where(lane8 >= 2 * edge * f, tile, aux_edge)
    edge_rows = T * 3 * tiles_per
    edge_right[edge_rows:, :] = aux_edge
    edge_left[edge_rows:, :] = aux_edge

    for block in (1, 0, 2):
        def go(block=block):
            edge_copy(True, block).start()
            edge_copy(False, block).start()
        if block == 1:
            go()
        else:
            pl.when(sends[0] if block == 0 else sends[1])(go)
    for g in range(early, groups):
        send_group(g)

    for copy in fetched[3:]:
        copy.wait()
    cells = cells_ref[...]
    slots = cells.shape[1]
    live = lax.broadcasted_iota(jnp.int32, (1, slots), 1) < count_ref[...]
    weight = jnp.where(live, 1.0, 0.0) / err_ref[...]
    square = weight * weight
    obs_row = jnp.zeros_like(cells)
    for r in range(1, band):
        obs_row = obs_row + jnp.where(cells >= r * lanes, 1, 0)
    obs_col = cells - lanes * obs_row
    row_hot = lax.broadcasted_iota(jnp.int32, (band, slots), 0) == obs_row
    sums = jnp.concatenate(
        [jnp.where(row_hot, square, 0.0), jnp.where(row_hot, square * vals_ref[...], 0.0)], 0
    )
    col_hot = jnp.where(lax.broadcasted_iota(jnp.int32, (lanes, slots), 0) == obs_col, 1.0, 0.0)
    sums = lax.dot_general(
        jnp.concatenate(split(sums, 3), 0), col_hot.astype(jnp.bfloat16), NT, preferred_element_type=jnp.float32
    )
    sums = (sums[4 * band :] + sums[2 * band : 4 * band]) + sums[: 2 * band]
    cell_weight, cell_value = sums[:band], sums[band:]

    half = 0.5 * TIME_STEP
    up_gain = jnp.where(has_up, half, 0.0).astype(jnp.float32)
    down_gain = jnp.where(has_dn, half, 0.0).astype(jnp.float32)

    def spread(tile):
        return jnp.concatenate([jnp.broadcast_to(tile[r : r + 1], (T, lanes)) for r in range(band)], 0)

    for side in range(2):
        @pl.when(receives[side])
        def _(side=side):
            aux_copy(side).wait_recv()
    aux_blocks = (aux_up, aux, aux_dn)
    coef = jnp.concatenate([half * spread(b[3 * band :, :]) for b in aux_blocks], 0)

    blocks = (up_buf, fac_ref, dn_buf)

    def take_group(g):
        for side in range(2):
            @pl.when(receives[side])
            def _(side=side):
                main_copy(side, g).wait_recv()
        state = []
        for f in range(3):
            loaded = [load(b, f, g) for b in blocks]
            state.append(jnp.concatenate(loaded, 0))
            for side in range(2):
                spot = (side * 3 + f,)
                tiles = roll(loaded[2 * side], slot * g + half_slot)
                if g > 0:
                    tiles = jnp.where(stack_lane >= slot * g, tiles, seam_buf[spot])
                seam_buf[spot] = tiles
        state = evolve(*state, coef, up_gain, down_gain, band)
        for f in range(3):
            for r in range(band):
                fc[f * band + r, T * g : T * (g + 1), :] = state[f][T * r : T * (r + 1)]

    for g in range(early):
        take_group(g)

    edge_copy(True, 1).wait_recv()
    edge_copy(False, 1).wait_recv()
    for side in range(2):
        @pl.when(receives[side])
        def _(side=side):
            edge_copy(True, 2 * side).wait_recv()
            edge_copy(False, 2 * side).wait_recv()

    def aux_pair(b, f):
        own = aux_blocks[b][f * band : (f + 1) * band, :]
        left = from_left[b, edge_rows:, :]
        right = from_right[b, edge_rows:, :]
        strips = jnp.where(lane8 < half_slot, roll(left, half_slot - edge - 2 * edge * f), roll(own, half_slot))
        strips = jnp.where(
            lane8 < slot,
            strips,
            jnp.where(lane8 < slot + half_slot, roll(own, slot + half_slot), roll(right, slot + half_slot - edge - 2 * edge * f)),
        )
        return own, strips

    def mean_group(b, f):
        own, strips = aux_pair(b, f)
        return jnp.concatenate([jnp.where(sub8 == 0, own[r : r + 1], strips[r : r + 1]) for r in range(band)], 0)

    mean_state = [jnp.concatenate([mean_group(b, f) for b in range(3)], 0) for f in range(4)]
    mean_state = evolve(*mean_state[:3], half * mean_state[3], up_gain, down_gain, band)
    mean = []
    for f in range(3):
        strips = roll(mean_state[f], -1, 0)
        low = roll(strips, -half_slot)
        high = roll(strips, lanes - half_slot - slot)
        mean.append(jnp.where(stack_lane < edge, low, jnp.where(stack_lane >= lanes - edge, high, mean_state[f])))

    def repeat_slots(tile):
        tile = jnp.where(lane8 < slot, tile, 0.0)
        total = tile
        for g in range(1, groups):
            total = total + roll(tile, slot * g)
        return total

    strips_of = [aux_pair(b, 3)[1] for b in range(3)]
    coef_left = jnp.concatenate([half * spread(repeat_slots(s)) for s in strips_of], 0)
    coef_right = jnp.concatenate([half * spread(repeat_slots(roll(s, -slot))) for s in strips_of], 0)

    for g in range(early, groups):
        take_group(g)

    def unpack(ref, b, f, first):
        out = []
        for r in range(band):
            row = T * (f * tiles_per + r // fold)
            out.append(roll(ref[b, row : row + T, :], first - edge * (r % fold)))
        return jnp.concatenate(out, 0)

    low_half = lax.rem(stack_lane, slot) < half_slot
    left_state, right_state = [], []
    for f in range(3):
        lefts, rights = [], []
        for b in range(3):
            seams = own_seams[f] if b == 1 else seam_buf[(b // 2) * 3 + f]
            lefts.append(jnp.where(low_half, unpack(from_left, b, f, half_slot - edge), seams))
            rights.append(jnp.where(low_half, seams, unpack(from_right, b, f, half_slot)))
        left_state.append(jnp.concatenate(lefts, 0))
        right_state.append(jnp.concatenate(rights, 0))
    left_state = evolve(*left_state, coef_left, up_gain, down_gain, band)
    right_state = evolve(*right_state, coef_right, up_gain, down_gain, band)
    at_edge = (lane8 < edge) | (lane8 >= lanes - edge)

    def merge(f):
        seams = jnp.where(low_half, right_state[f], left_state[f])
        for g in range(groups):
            back = roll(seams, -(slot * g + half_slot))
            for r in range(band):
                spot = (f * band + r, slice(T * g, T * (g + 1)), slice(None))
                fc[spot] = jnp.where(at_edge, back[T * r : T * (r + 1)], fc[spot])

    merge(0)
    lhs, rhs = [], []
    for r in range(band):
        height = fc[r]
        w = cell_weight[r : r + 1]
        drive = cell_value[r : r + 1] - w * mean[0][T * r : T * r + 1]
        lhs.append(height)
        pad = jnp.zeros((lanes // 2 - rank - T, lanes), jnp.float32)
        rhs.append(jnp.concatenate([height * w, jnp.where(sub8 == 0, drive, 0.0), pad], 0))
    gram = lax.dot_general(
        jnp.concatenate(split(jnp.concatenate(lhs, 1), 2), 0),
        jnp.concatenate(split(jnp.concatenate(rhs, 1), 2), 0),
        NT, preferred_element_type=jnp.float32,
    )
    gram = gram[:rank] + gram[rank:]
    gram = gram + roll(gram, lanes // 2)
    hr = rank // 2
    wide = lax.broadcasted_iota(jnp.int32, (hr, lanes), 1)
    mine = jnp.where(wide < lanes // 2, gram[:hr], gram[hr:])

    gram_out[...] = mine
    merge(1)
    merge(2)
    for f in range(3):
        for r in range(band):
            mean_out[f * band + r : f * band + r + 1, :] = mean[f][T * r : T * r + 1]
    for side in range(2):
        @pl.when(sends[side])
        def _(side=side):
            aux_copy(side).wait_send()
            for g in range(groups):
                main_copy(side, g).wait_send()
            edge_copy(True, 2 * side).wait_send()
            edge_copy(False, 2 * side).wait_send()
    edge_copy(True, 1).wait_send()
    edge_copy(False, 1).wait_send()

def total(n_lat, n_lon, part_ref, sum_ref, mid, ar1, ar2, s1, r1, s2, r2):
    lat, lon = lax.axis_index("lat"), lax.axis_index("lon")

    def at(dlat, dlon):
        return (lax.rem(lat + dlat, n_lat), lax.rem(lon + dlon, n_lon))

    barrier = pltpu.get_barrier_semaphore()
    for o in range(1, n_lat):
        pl.semaphore_signal(barrier, inc=1, device_id=at(o, 0), device_id_type=MESH)
    for o in range(1, n_lon):
        pl.semaphore_signal(barrier, inc=1, device_id=at(0, o), device_id_type=MESH)
    pl.semaphore_wait(barrier, n_lat + n_lon - 2)

    def exchange(src, slots, ssem, rsem, count, step):
        copies = [
            pltpu.make_async_remote_copy(
                src_ref=src, dst_ref=slots.at[o - 1], send_sem=ssem.at[o - 1], recv_sem=rsem.at[o - 1],
                device_id=at(o * step[0], o * step[1]), device_id_type=MESH,
            )
            for o in range(1, count)
        ]
        for copy in copies:
            copy.start()
        mine = src[...]
        for o, copy in enumerate(copies):
            copy.wait_recv()
            mine = mine + slots[o]
        return mine, copies

    mid[...], first = exchange(part_ref, ar1, s1, r1, n_lat, (1, 0))
    sum_ref[...], second = exchange(mid, ar2, s2, r2, n_lon, (0, 1))
    for copy in first + second:
        copy.wait_send()


def transform(rank, fc, mean_ref, gram_ref, upd_hbm, out_hbm, upd, res, s_out):
    mine = gram_ref[...]
    lanes = mine.shape[1]
    band = fc.shape[0] // 3
    groups = rank // T
    sub8 = lax.broadcasted_iota(jnp.int32, (T, lanes), 0)
    both = jnp.concatenate([mine, roll(mine, lanes // 2)], 0)
    ri = lax.broadcasted_iota(jnp.int32, (rank, lanes), 0)
    li = lax.broadcasted_iota(jnp.int32, (rank, lanes), 1)
    eyes = jnp.where((li == ri) | (li == ri + lanes // 2), 1.0, 0.0)
    x = jnp.where(li < lanes // 2, both, 0.0) + eyes
    tiles = [x[T * i : T * (i + 1)] for i in range(groups)]
    for b in range(groups):
        cols = {
            (i, q): jnp.broadcast_to(tiles[i][:, T * b + q : T * b + q + 1], (T, lanes))
            for i in range(b, groups)
            for q in range(T)
        }
        for q in range(T):
            inv = 1.0 / cols[b, q][q : q + 1]
            row = tiles[b][q : q + 1]
            heads = [cols[b, p][q : q + 1] for p in range(q + 1, T)]
            for i in range(b, groups):
                if i == b and q == T - 1:
                    continue
                m = cols[i, q] * inv
                if i == b:
                    m = jnp.where(sub8 > q, m, 0.0)
                for p in range(q + 1, T):
                    cols[i, p] = cols[i, p] - m * heads[p - q - 1]
                tiles[i] = tiles[i] - m * row
    x = jnp.concatenate(tiles, 0)
    pivot = jnp.sum(jnp.where(li == ri, x, 0.0), 1, keepdims=True)
    x = x / jnp.sqrt(pivot)
    inverse = jnp.where(li < rank, roll(x, -(lanes // 2)), 0.0)
    z = x[:, rank : rank + 1]
    shift = jnp.sum(inverse * z, 0, keepdims=True)
    coefs = jnp.concatenate([inverse, jnp.where(sub8 == 0, shift, 0.0)], 0)
    high, low = (c.astype(jnp.float32) for c in split(coefs, 2))
    stacked = (high + roll(high, rank) + roll(low, 2 * rank))[:, : 3 * rank].astype(jnp.bfloat16)

    per = 3 * band
    for f in range(3):
        slab = jnp.concatenate([fc[f * band + r] for r in range(band)], 1)
        high, low = split(slab, 2)
        part = jnp.dot(stacked, jnp.concatenate([high, low, high], 0), preferred_element_type=jnp.float32)
        for r in range(band):
            col = part[:, lanes * r : lanes * (r + 1)]
            i = f * band + r
            for g in range(groups):
                res[pl.ds(g * T * per + i, T, stride=per), :] = col[T * g : T * (g + 1)]
            upd[i : i + 1, :] = mean_ref[i : i + 1, :] + col[rank : rank + 1]
    copies = [
        pltpu.make_async_copy(res, out_hbm, s_out.at[0]),
        pltpu.make_async_copy(upd, upd_hbm, s_out.at[1]),
    ]
    for copy in copies:
        copy.start()
    for copy in copies:
        copy.wait()


def in_hbm(x):
    return pltpu.with_memory_space_constraint(x, pltpu.HBM)


def per_device(n_lat, n_lon, background, factor, depth, cells, count, values, error):
    rank, fields, band, lanes = factor.shape
    groups = rank // T
    rows = rank * fields * band
    slots = cells.shape[0]
    assert band == T and 2 * STEPS <= band and rank % T == 0 and fields == 3
    edge_rows = T * (fields * band * groups * 2 * STEPS // lanes + 1)
    vmem = pl.BlockSpec(memory_space=pltpu.VMEM)
    f32 = functools.partial(pltpu.VMEM, dtype=jnp.float32)
    dma = pltpu.SemaphoreType.DMA
    anywhere = pl.BlockSpec(memory_space=pl.ANY)
    forecast, mean, gram = pl.pallas_call(
        functools.partial(kernel, n_lat, n_lon, rank),
        out_shape=(
            jax.ShapeDtypeStruct((fields * band, rank, lanes), jnp.float32),
            jax.ShapeDtypeStruct((fields * band, lanes), jnp.float32),
            jax.ShapeDtypeStruct((rank // 2, lanes), jnp.float32),
        ),
        in_specs=[pl.BlockSpec(memory_space=pltpu.HBM)] * 7,
        out_specs=(vmem, vmem, vmem),
        scratch_shapes=[
            f32((rows, lanes)), pltpu.VMEM((1, slots), jnp.int32), pltpu.VMEM((1, 1), jnp.int32),
            f32((1, slots)), f32((1, slots)), dma((7,)),
            f32((rows, lanes)), f32((rows, lanes)),
            f32((4 * band, lanes)), f32((4 * band, lanes)), f32((4 * band, lanes)),
            f32((edge_rows, lanes)), f32((edge_rows, lanes)),
            f32((3, edge_rows, lanes)), f32((3, edge_rows, lanes)),
            f32((2 * fields, T * band, lanes)),
            dma((2, groups)), dma((2, groups)), dma((2,)), dma((2,)),
            dma((3,)), dma((3,)), dma((3,)), dma((3,)),
        ],
        compiler_params=pltpu.CompilerParams(
            collective_id=0, has_side_effects=True, vmem_limit_bytes=32 * 1024 * 1024
        ),
    )(
        in_hbm(background.reshape(fields * band, lanes)), in_hbm(factor.reshape(rows, lanes)), in_hbm(depth),
        in_hbm(cells.reshape(1, slots)), count.reshape(1, 1), in_hbm(values.reshape(1, slots)), in_hbm(error.reshape(1, slots)),
    )
    gram = pl.pallas_call(
        functools.partial(total, n_lat, n_lon),
        out_shape=jax.ShapeDtypeStruct(gram.shape, jnp.float32),
        in_specs=[vmem],
        out_specs=vmem,
        scratch_shapes=[
            f32(gram.shape), f32((n_lat - 1, *gram.shape)), f32((n_lon - 1, *gram.shape)),
            dma((n_lat - 1,)), dma((n_lat - 1,)), dma((n_lon - 1,)), dma((n_lon - 1,)),
        ],
        compiler_params=pltpu.CompilerParams(
            collective_id=1, has_side_effects=True, vmem_limit_bytes=4 * 1024 * 1024
        ),
    )(gram)
    updated, analysis = pl.pallas_call(
        functools.partial(transform, rank),
        out_shape=(
            jax.ShapeDtypeStruct((fields * band, lanes), jnp.float32),
            jax.ShapeDtypeStruct((rows, lanes), jnp.float32),
        ),
        in_specs=[vmem] * 3,
        out_specs=(anywhere, anywhere),
        scratch_shapes=[f32((fields * band, lanes)), f32((rows, lanes)), dma((2,))],
        compiler_params=pltpu.CompilerParams(vmem_limit_bytes=16 * 1024 * 1024),
    )(forecast, mean, gram)
    return updated.reshape(background.shape), analysis.reshape(factor.shape)


def solution(mesh):
    return jax.shard_map(
        functools.partial(per_device, mesh.shape["lat"], mesh.shape["lon"]),
        mesh=mesh,
        in_specs=(
            P(None, "lat", "lon"),
            P(None, None, "lat", "lon"),
            P("lat", "lon"),
            P(("lat", "lon")),
            P(("lat", "lon")),
            P(("lat", "lon")),
            P(("lat", "lon")),
        ),
        out_specs=(P(None, "lat", "lon"), P(None, None, "lat", "lon")),
        check_vma=False,
    )
```

```python
import functools

import jax
import jax.numpy as jnp
from jax import lax
from jax.experimental import pallas as pl
from jax.experimental.pallas import tpu as pltpu
from jax.sharding import PartitionSpec as P

STEPS = 4
TIME_STEP = 0.9
ROTATION = 0.25
MESH = pl.DeviceIdType.MESH
T = 8
NT = (((1,), (1,)), ((), ()))


def roll(x, shift, axis=1):
    shift = shift % x.shape[axis]
    return x if shift == 0 else pltpu.roll(x, shift, axis)


def split(x, terms):
    parts = []
    for _ in range(terms):
        part = x.astype(jnp.bfloat16)
        parts.append(part)
        x = x - part.astype(jnp.float32)
    return parts


def evolve(h, e, n, coef, up_gain, down_gain, band):
    half = 0.5 * TIME_STEP
    for step in range(STEPS):
        w = 2 * (STEPS - step)
        last = coef.shape[0] - T * (band - w + 1)
        mid = e[T:-T]
        div = (roll(mid, -1) - roll(mid, 1)) + (n[2 * T :] - n[: -2 * T])
        hn = h[T:-T] - coef[T * (band - w + 1) : last] * div
        inner = hn[T:-T]
        shape = (T * (w - 2), h.shape[1])
        parts = [jnp.full((T * band, h.shape[1]), half, jnp.float32)]
        if w > 2:
            parts = [jnp.full(shape, up_gain)] + parts + [jnp.full(shape, down_gain)]
        gain = jnp.concatenate(parts, 0) if w > 2 else parts[0]
        e0, n0 = e[2 * T : -2 * T], n[2 * T : -2 * T]
        e = e0 - half * (roll(inner, -1) - roll(inner, 1)) + ROTATION * n0
        n = n0 - gain * (hn[2 * T :] - hn[: -2 * T]) - ROTATION * e0
        h = inner
    return h, e, n


def pair_of(n_lon):
    return 2 if n_lon % 2 == 0 else 1


def kernel(
    n_lat, n_lon, rank,
    mean_hbm, fac_hbm, depth_hbm, cells_hbm, count_hbm, vals_hbm, err_hbm,
    fc, mean_out, gram_out,
    fac_ref, cells_ref, count_ref, vals_ref, err_ref, s_in,
    up_buf, dn_buf, aux, aux_up, aux_dn, edge_right, edge_left, from_left, from_right,
    seam_buf, p1, p2, ar1, ar2,
    s_main, r_main, s_aux, r_aux, s_el, r_el, s_er, r_er, s1, r1, s2, r2,
):
    lat, lon = lax.axis_index("lat"), lax.axis_index("lon")
    band, lanes = depth_hbm.shape
    groups = rank // T
    slot = lanes // groups
    half_slot = slot // 2
    edge = 2 * STEPS
    per = 3 * band
    chunk = T * per
    lane8 = lax.broadcasted_iota(jnp.int32, (T, lanes), 1)
    sub8 = lax.broadcasted_iota(jnp.int32, (T, lanes), 0)

    def at(dlat, dlon):
        return (lax.rem(lat + dlat + n_lat, n_lat), lax.rem(lon + dlon + n_lon, n_lon))

    inner = pair_of(n_lon)
    outer, plane = n_lon // inner, n_lat * inner
    lon_in, lon_out = lax.rem(lon, inner), lon // inner
    place = lat * inner + lon_in

    def in_plane(o):
        peer = lax.rem(place + o, plane)
        return (peer // inner, lon_out * inner + lax.rem(peer, inner))

    def in_line(o):
        return (lat, lax.rem(lon_out + o, outer) * inner + lon_in)

    if inner == 2:
        beyond = 2 * lon_in - 1
        rest = [at(a, beyond) for a in (0, -1, 1)]
    else:
        rest = [at(a, b) for a in (-1, 1) for b in (-1, 1)]
    peers = [in_plane(o) for o in range(1, plane)] + rest + [in_line(o) for o in range(1, outer)]
    barrier = pltpu.get_barrier_semaphore()
    for peer in peers:
        pl.semaphore_signal(barrier, inc=1, device_id=peer, device_id_type=MESH)

    has_up, has_dn = lat > 0, lat < n_lat - 1
    fetched = [
        pltpu.make_async_copy(src, dst, s_in.at[i])
        for i, (src, dst) in enumerate((
            (mean_hbm, aux.at[pl.ds(0, 3 * band)]),
            (depth_hbm, aux.at[pl.ds(3 * band, band)]),
            (fac_hbm, fac_ref),
            (cells_hbm, cells_ref),
            (count_hbm, count_ref),
            (vals_hbm, vals_ref),
            (err_hbm, err_ref),
        ))
    ]
    for copy in fetched:
        copy.start()

    @pl.when(jnp.logical_not(has_up))
    def _():
        up_buf[...] = jnp.zeros_like(up_buf)
        aux_up[...] = jnp.zeros_like(aux_up)
        from_left[0] = jnp.zeros_like(from_left[0])
        from_right[0] = jnp.zeros_like(from_right[0])

    @pl.when(jnp.logical_not(has_dn))
    def _():
        dn_buf[...] = jnp.zeros_like(dn_buf)
        aux_dn[...] = jnp.zeros_like(aux_dn)
        from_left[2] = jnp.zeros_like(from_left[2])
        from_right[2] = jnp.zeros_like(from_right[2])

    def remote(src, dst, ssem, rsem, where):
        return pltpu.make_async_remote_copy(
            src_ref=src, dst_ref=dst, send_sem=ssem, recv_sem=rsem, device_id=where, device_id_type=MESH
        )

    def main_copy(side, g):
        rows = pl.ds(g * chunk, chunk)
        dst = (up_buf, dn_buf)[side]
        return remote(fac_hbm.at[rows], dst.at[rows], s_main.at[side, g], r_main.at[side, g], at(1 - 2 * side, 0))

    def aux_copy(side):
        dst = (aux_up, aux_dn)[side]
        return remote(aux, dst, s_aux.at[side], r_aux.at[side], at(1 - 2 * side, 0))

    def edge_copy(to_right, block):
        dlat = 1 - block
        if to_right:
            return remote(edge_right, from_left.at[block], s_er.at[block], r_er.at[block], at(dlat, 1))
        return remote(edge_left, from_right.at[block], s_el.at[block], r_el.at[block], at(dlat, -1))

    sends = (has_dn, has_up)
    receives = (has_up, has_dn)

    pl.semaphore_wait(barrier, len(peers))
    fetched[0].wait()
    fetched[1].wait()

    def send_group(g):
        for side in range(2):
            @pl.when(sends[side])
            def _(side=side):
                main_copy(side, g).start()

    for side in range(2):
        @pl.when(sends[side])
        def _(side=side):
            aux_copy(side).start()
    early = groups // 2
    for g in range(early):
        send_group(g)

    def load(ref, f, g):
        return jnp.concatenate([ref[pl.ds(g * chunk + f * band + r, T, stride=per), :] for r in range(band)], 0)

    stack_lane = lax.broadcasted_iota(jnp.int32, (T * band, lanes), 1)
    stack_sub = lax.broadcasted_iota(jnp.int32, (T * band, lanes), 0)

    def seam_tiles(ref, f):
        tiles = roll(load(ref, f, groups - 1), slot * (groups - 1) + half_slot)
        for g in range(groups - 1):
            tiles = jnp.where(
                (stack_lane >= slot * g) & (stack_lane < slot * (g + 1)),
                roll(load(ref, f, g), slot * g + half_slot),
                tiles,
            )
        return tiles

    fetched[2].wait()
    fold = slot // edge
    own_seams = []
    tiles_per = band // fold
    in_slot = lax.rem(lane8, slot)
    for f in range(3):
        seams = seam_tiles(fac_ref, f)
        own_seams.append(seams)
        for t in range(tiles_per):
            right = left = None
            for q in range(fold):
                tile = seams[T * (t * fold + q) : T * (t * fold + q + 1)]
                to_right = roll(tile, edge * q - (half_slot - edge))
                to_left = roll(tile, edge * q - half_slot)
                keep = (in_slot >= edge * q) & (in_slot < edge * (q + 1))
                right = to_right if q == 0 else jnp.where(keep, to_right, right)
                left = to_left if q == 0 else jnp.where(keep, to_left, left)
            row = T * (f * tiles_per + t)
            edge_right[row : row + T, :] = right
            edge_left[row : row + T, :] = left
    aux_edge = None
    for f in range(4):
        tile = roll(aux[f * band : (f + 1) * band, :], 2 * edge * f + edge)
        aux_edge = tile if f == 0 else jnp.where(lane8 >= 2 * edge * f, tile, aux_edge)
    edge_rows = T * 3 * tiles_per
    edge_right[edge_rows:, :] = aux_edge
    edge_left[edge_rows:, :] = aux_edge

    for block in (1, 0, 2):
        def go(block=block):
            edge_copy(True, block).start()
            edge_copy(False, block).start()
        if block == 1:
            go()
        else:
            pl.when(sends[0] if block == 0 else sends[1])(go)
    for g in range(early, groups):
        send_group(g)

    for copy in fetched[3:]:
        copy.wait()
    cells = cells_ref[...]
    slots = cells.shape[1]
    live = lax.broadcasted_iota(jnp.int32, (1, slots), 1) < count_ref[...]
    weight = jnp.where(live, 1.0, 0.0) / err_ref[...]
    square = weight * weight
    obs_row = jnp.zeros_like(cells)
    for r in range(1, band):
        obs_row = obs_row + jnp.where(cells >= r * lanes, 1, 0)
    obs_col = cells - lanes * obs_row
    row_hot = lax.broadcasted_iota(jnp.int32, (band, slots), 0) == obs_row
    sums = jnp.concatenate(
        [jnp.where(row_hot, square, 0.0), jnp.where(row_hot, square * vals_ref[...], 0.0)], 0
    )
    col_hot = jnp.where(lax.broadcasted_iota(jnp.int32, (lanes, slots), 0) == obs_col, 1.0, 0.0)
    sums = lax.dot_general(
        jnp.concatenate(split(sums, 3), 0), col_hot.astype(jnp.bfloat16), NT, preferred_element_type=jnp.float32
    )
    sums = (sums[4 * band :] + sums[2 * band : 4 * band]) + sums[: 2 * band]
    cell_weight, cell_value = sums[:band], sums[band:]

    half = 0.5 * TIME_STEP
    up_gain = jnp.where(has_up, half, 0.0).astype(jnp.float32)
    down_gain = jnp.where(has_dn, half, 0.0).astype(jnp.float32)

    def spread(tile):
        return jnp.concatenate([jnp.broadcast_to(tile[r : r + 1], (T, lanes)) for r in range(band)], 0)

    for side in range(2):
        @pl.when(receives[side])
        def _(side=side):
            aux_copy(side).wait_recv()
    aux_blocks = (aux_up, aux, aux_dn)
    coef = jnp.concatenate([half * spread(b[3 * band :, :]) for b in aux_blocks], 0)

    blocks = (up_buf, fac_ref, dn_buf)

    def take_group(g):
        for side in range(2):
            @pl.when(receives[side])
            def _(side=side):
                main_copy(side, g).wait_recv()
        state = []
        for f in range(3):
            loaded = [load(b, f, g) for b in blocks]
            state.append(jnp.concatenate(loaded, 0))
            for side in range(2):
                spot = (side * 3 + f,)
                tiles = roll(loaded[2 * side], slot * g + half_slot)
                if g > 0:
                    tiles = jnp.where(stack_lane >= slot * g, tiles, seam_buf[spot])
                seam_buf[spot] = tiles
        state = evolve(*state, coef, up_gain, down_gain, band)
        for f in range(3):
            for r in range(band):
                fc[f * band + r, T * g : T * (g + 1), :] = state[f][T * r : T * (r + 1)]

    for g in range(early):
        take_group(g)

    edge_copy(True, 1).wait_recv()
    edge_copy(False, 1).wait_recv()
    for side in range(2):
        @pl.when(receives[side])
        def _(side=side):
            edge_copy(True, 2 * side).wait_recv()
            edge_copy(False, 2 * side).wait_recv()

    def aux_pair(b, f):
        own = aux_blocks[b][f * band : (f + 1) * band, :]
        left = from_left[b, edge_rows:, :]
        right = from_right[b, edge_rows:, :]
        strips = jnp.where(lane8 < half_slot, roll(left, half_slot - edge - 2 * edge * f), roll(own, half_slot))
        strips = jnp.where(
            lane8 < slot,
            strips,
            jnp.where(lane8 < slot + half_slot, roll(own, slot + half_slot), roll(right, slot + half_slot - edge - 2 * edge * f)),
        )
        return own, strips

    def mean_group(b, f):
        own, strips = aux_pair(b, f)
        return jnp.concatenate([jnp.where(sub8 == 0, own[r : r + 1], strips[r : r + 1]) for r in range(band)], 0)

    mean_state = [jnp.concatenate([mean_group(b, f) for b in range(3)], 0) for f in range(4)]
    mean_state = evolve(*mean_state[:3], half * mean_state[3], up_gain, down_gain, band)
    mean = []
    for f in range(3):
        strips = roll(mean_state[f], -1, 0)
        low = roll(strips, -half_slot)
        high = roll(strips, lanes - half_slot - slot)
        mean.append(jnp.where(stack_lane < edge, low, jnp.where(stack_lane >= lanes - edge, high, mean_state[f])))

    def repeat_slots(tile):
        tile = jnp.where(lane8 < slot, tile, 0.0)
        total = tile
        for g in range(1, groups):
            total = total + roll(tile, slot * g)
        return total

    strips_of = [aux_pair(b, 3)[1] for b in range(3)]
    coef_left = jnp.concatenate([half * spread(repeat_slots(s)) for s in strips_of], 0)
    coef_right = jnp.concatenate([half * spread(repeat_slots(roll(s, -slot))) for s in strips_of], 0)

    for g in range(early, groups):
        take_group(g)

    def unpack(ref, b, f, first):
        out = []
        for r in range(band):
            row = T * (f * tiles_per + r // fold)
            out.append(roll(ref[b, row : row + T, :], first - edge * (r % fold)))
        return jnp.concatenate(out, 0)

    low_half = lax.rem(stack_lane, slot) < half_slot
    left_state, right_state = [], []
    for f in range(3):
        lefts, rights = [], []
        for b in range(3):
            seams = own_seams[f] if b == 1 else seam_buf[(b // 2) * 3 + f]
            lefts.append(jnp.where(low_half, unpack(from_left, b, f, half_slot - edge), seams))
            rights.append(jnp.where(low_half, seams, unpack(from_right, b, f, half_slot)))
        left_state.append(jnp.concatenate(lefts, 0))
        right_state.append(jnp.concatenate(rights, 0))
    left_state = evolve(*left_state, coef_left, up_gain, down_gain, band)
    right_state = evolve(*right_state, coef_right, up_gain, down_gain, band)
    at_edge = (lane8 < edge) | (lane8 >= lanes - edge)

    def merge(f):
        seams = jnp.where(low_half, right_state[f], left_state[f])
        for g in range(groups):
            back = roll(seams, -(slot * g + half_slot))
            for r in range(band):
                spot = (f * band + r, slice(T * g, T * (g + 1)), slice(None))
                fc[spot] = jnp.where(at_edge, back[T * r : T * (r + 1)], fc[spot])

    merge(0)
    lhs, rhs = [], []
    for r in range(band):
        height = fc[r]
        w = cell_weight[r : r + 1]
        drive = cell_value[r : r + 1] - w * mean[0][T * r : T * r + 1]
        lhs.append(height)
        pad = jnp.zeros((lanes // 2 - rank - T, lanes), jnp.float32)
        rhs.append(jnp.concatenate([height * w, jnp.where(sub8 == 0, drive, 0.0), pad], 0))
    gram = lax.dot_general(
        jnp.concatenate(split(jnp.concatenate(lhs, 1), 2), 0),
        jnp.concatenate(split(jnp.concatenate(rhs, 1), 2), 0),
        NT, preferred_element_type=jnp.float32,
    )
    gram = gram[:rank] + gram[rank:]
    gram = gram + roll(gram, lanes // 2)
    hr = rank // 2
    wide = lax.broadcasted_iota(jnp.int32, (hr, lanes), 1)
    mine = jnp.where(wide < lanes // 2, gram[:hr], gram[hr:])

    p1[...] = mine
    def lat_copy(o):
        return remote(p1, ar1.at[o - 1], s1.at[o - 1], r1.at[o - 1], in_plane(o))
    def lon_copy(o):
        return remote(p2, ar2.at[o - 1], s2.at[o - 1], r2.at[o - 1], in_line(o))
    for o in range(1, plane):
        lat_copy(o).start()
    merge(1)
    merge(2)
    for f in range(3):
        for r in range(band):
            mean_out[f * band + r : f * band + r + 1, :] = mean[f][T * r : T * r + 1]
    for o in range(1, plane):
        lat_copy(o).wait_recv()
        mine = mine + ar1[o - 1]
    p2[...] = mine
    for o in range(1, outer):
        lon_copy(o).start()
    for o in range(1, outer):
        lon_copy(o).wait_recv()
        mine = mine + ar2[o - 1]

    gram_out[...] = mine

    for side in range(2):
        @pl.when(sends[side])
        def _(side=side):
            aux_copy(side).wait_send()
            for g in range(groups):
                main_copy(side, g).wait_send()
            edge_copy(True, 2 * side).wait_send()
            edge_copy(False, 2 * side).wait_send()
    edge_copy(True, 1).wait_send()
    edge_copy(False, 1).wait_send()
    for o in range(1, plane):
        lat_copy(o).wait_send()
    for o in range(1, outer):
        lon_copy(o).wait_send()


def transform(rank, fc, mean_ref, gram_ref, upd_hbm, out_hbm, upd, res, s_out):
    mine = gram_ref[...]
    lanes = mine.shape[1]
    band = fc.shape[0] // 3
    groups = rank // T
    sub8 = lax.broadcasted_iota(jnp.int32, (T, lanes), 0)
    both = jnp.concatenate([mine, roll(mine, lanes // 2)], 0)
    ri = lax.broadcasted_iota(jnp.int32, (rank, lanes), 0)
    li = lax.broadcasted_iota(jnp.int32, (rank, lanes), 1)
    eyes = jnp.where((li == ri) | (li == ri + lanes // 2), 1.0, 0.0)
    x = jnp.where(li < lanes // 2, both, 0.0) + eyes
    tiles = [x[T * i : T * (i + 1)] for i in range(groups)]
    for b in range(groups):
        cols = {
            (i, q): jnp.broadcast_to(tiles[i][:, T * b + q : T * b + q + 1], (T, lanes))
            for i in range(b, groups)
            for q in range(T)
        }
        for q in range(T):
            inv = 1.0 / cols[b, q][q : q + 1]
            row = tiles[b][q : q + 1]
            heads = [cols[b, p][q : q + 1] for p in range(q + 1, T)]
            for i in range(b, groups):
                if i == b and q == T - 1:
                    continue
                m = cols[i, q] * inv
                if i == b:
                    m = jnp.where(sub8 > q, m, 0.0)
                for p in range(q + 1, T):
                    cols[i, p] = cols[i, p] - m * heads[p - q - 1]
                tiles[i] = tiles[i] - m * row
    x = jnp.concatenate(tiles, 0)
    pivot = jnp.sum(jnp.where(li == ri, x, 0.0), 1, keepdims=True)
    x = x / jnp.sqrt(pivot)
    inverse = jnp.where(li < rank, roll(x, -(lanes // 2)), 0.0)
    z = x[:, rank : rank + 1]
    shift = jnp.sum(inverse * z, 0, keepdims=True)
    coefs = jnp.concatenate([inverse, jnp.where(sub8 == 0, shift, 0.0)], 0)
    high, low = (c.astype(jnp.float32) for c in split(coefs, 2))
    stacked = (high + roll(high, rank) + roll(low, 2 * rank))[:, : 3 * rank].astype(jnp.bfloat16)

    per = 3 * band
    for f in range(3):
        slab = jnp.concatenate([fc[f * band + r] for r in range(band)], 1)
        high, low = split(slab, 2)
        part = jnp.dot(stacked, jnp.concatenate([high, low, high], 0), preferred_element_type=jnp.float32)
        for r in range(band):
            col = part[:, lanes * r : lanes * (r + 1)]
            i = f * band + r
            for g in range(groups):
                res[pl.ds(g * T * per + i, T, stride=per), :] = col[T * g : T * (g + 1)]
            upd[i : i + 1, :] = mean_ref[i : i + 1, :] + col[rank : rank + 1]
    copies = [
        pltpu.make_async_copy(res, out_hbm, s_out.at[0]),
        pltpu.make_async_copy(upd, upd_hbm, s_out.at[1]),
    ]
    for copy in copies:
        copy.start()
    for copy in copies:
        copy.wait()


def in_hbm(x):
    return pltpu.with_memory_space_constraint(x, pltpu.HBM)


def per_device(n_lat, n_lon, background, factor, depth, cells, count, values, error):
    rank, fields, band, lanes = factor.shape
    groups = rank // T
    rows = rank * fields * band
    slots = cells.shape[0]
    assert band == T and 2 * STEPS <= band and rank % T == 0 and fields == 3
    plane, outer = n_lat * pair_of(n_lon), n_lon // pair_of(n_lon)
    edge_rows = T * (fields * band * groups * 2 * STEPS // lanes + 1)
    vmem = pl.BlockSpec(memory_space=pltpu.VMEM)
    f32 = functools.partial(pltpu.VMEM, dtype=jnp.float32)
    dma = pltpu.SemaphoreType.DMA
    anywhere = pl.BlockSpec(memory_space=pl.ANY)
    forecast, mean, gram = pl.pallas_call(
        functools.partial(kernel, n_lat, n_lon, rank),
        out_shape=(
            jax.ShapeDtypeStruct((fields * band, rank, lanes), jnp.float32),
            jax.ShapeDtypeStruct((fields * band, lanes), jnp.float32),
            jax.ShapeDtypeStruct((rank // 2, lanes), jnp.float32),
        ),
        in_specs=[pl.BlockSpec(memory_space=pltpu.HBM)] * 7,
        out_specs=(vmem, vmem, vmem),
        scratch_shapes=[
            f32((rows, lanes)), pltpu.VMEM((1, slots), jnp.int32), pltpu.VMEM((1, 1), jnp.int32),
            f32((1, slots)), f32((1, slots)), dma((7,)),
            f32((rows, lanes)), f32((rows, lanes)),
            f32((4 * band, lanes)), f32((4 * band, lanes)), f32((4 * band, lanes)),
            f32((edge_rows, lanes)), f32((edge_rows, lanes)),
            f32((3, edge_rows, lanes)), f32((3, edge_rows, lanes)),
            f32((2 * fields, T * band, lanes)), f32((rank // 2, lanes)), f32((rank // 2, lanes)),
            f32((plane - 1, rank // 2, lanes)), f32((outer - 1, rank // 2, lanes)),
            dma((2, groups)), dma((2, groups)), dma((2,)), dma((2,)),
            dma((3,)), dma((3,)), dma((3,)), dma((3,)),
            dma((plane - 1,)), dma((plane - 1,)), dma((outer - 1,)), dma((outer - 1,)),
        ],
        compiler_params=pltpu.CompilerParams(
            collective_id=0, has_side_effects=True, vmem_limit_bytes=32 * 1024 * 1024
        ),
    )(
        in_hbm(background.reshape(fields * band, lanes)), in_hbm(factor.reshape(rows, lanes)), in_hbm(depth),
        in_hbm(cells.reshape(1, slots)), count.reshape(1, 1), in_hbm(values.reshape(1, slots)), in_hbm(error.reshape(1, slots)),
    )
    updated, analysis = pl.pallas_call(
        functools.partial(transform, rank),
        out_shape=(
            jax.ShapeDtypeStruct((fields * band, lanes), jnp.float32),
            jax.ShapeDtypeStruct((rows, lanes), jnp.float32),
        ),
        in_specs=[vmem] * 3,
        out_specs=(anywhere, anywhere),
        scratch_shapes=[f32((fields * band, lanes)), f32((rows, lanes)), dma((2,))],
        compiler_params=pltpu.CompilerParams(vmem_limit_bytes=16 * 1024 * 1024),
    )(forecast, mean, gram)
    return updated.reshape(background.shape), analysis.reshape(factor.shape)


def solution(mesh):
    return jax.shard_map(
        functools.partial(per_device, mesh.shape["lat"], mesh.shape["lon"]),
        mesh=mesh,
        in_specs=(
            P(None, "lat", "lon"),
            P(None, None, "lat", "lon"),
            P("lat", "lon"),
            P(("lat", "lon")),
            P(("lat", "lon")),
            P(("lat", "lon")),
            P(("lat", "lon")),
        ),
        out_specs=(P(None, "lat", "lon"), P(None, None, "lat", "lon")),
        check_vma=False,
    )
```

```python
import functools

import jax
import jax.numpy as jnp
from jax import lax
from jax.experimental import pallas as pl
from jax.experimental.pallas import tpu as pltpu
from jax.sharding import PartitionSpec as P

STEPS = 4
TIME_STEP = 0.9
ROTATION = 0.25
MESH = pl.DeviceIdType.MESH
T = 8
NT = (((1,), (1,)), ((), ()))


def roll(x, shift, axis=1):
    shift = shift % x.shape[axis]
    return x if shift == 0 else pltpu.roll(x, shift, axis)


def split(x, terms):
    parts = []
    for _ in range(terms):
        part = x.astype(jnp.bfloat16)
        parts.append(part)
        x = x - part.astype(jnp.float32)
    return parts


def evolve(h, e, n, coef, up_gain, down_gain, band):
    half = 0.5 * TIME_STEP
    for step in range(STEPS):
        w = 2 * (STEPS - step)
        last = coef.shape[0] - T * (band - w + 1)
        mid = e[T:-T]
        div = (roll(mid, -1) - roll(mid, 1)) + (n[2 * T :] - n[: -2 * T])
        hn = h[T:-T] - coef[T * (band - w + 1) : last] * div
        inner = hn[T:-T]
        shape = (T * (w - 2), h.shape[1])
        parts = [jnp.full((T * band, h.shape[1]), half, jnp.float32)]
        if w > 2:
            parts = [jnp.full(shape, up_gain)] + parts + [jnp.full(shape, down_gain)]
        gain = jnp.concatenate(parts, 0) if w > 2 else parts[0]
        e0, n0 = e[2 * T : -2 * T], n[2 * T : -2 * T]
        e = e0 - half * (roll(inner, -1) - roll(inner, 1)) + ROTATION * n0
        n = n0 - gain * (hn[2 * T :] - hn[: -2 * T]) - ROTATION * e0
        h = inner
    return h, e, n


def kernel(
    n_lat, n_lon, rank,
    mean_hbm, fac_hbm, depth_hbm, cells_hbm, count_hbm, vals_hbm, err_hbm,
    fc, mean_out, gram_out,
    fac_ref, cells_ref, count_ref, vals_ref, err_ref, s_in,
    up_buf, dn_buf, aux, aux_up, aux_dn, edge_right, edge_left, from_left, from_right,
    p1, p2, ar1, ar2,
    s_main, r_main, s_aux, r_aux, s_el, r_el, s_er, r_er, s1, r1, s2, r2,
):
    lat, lon = lax.axis_index("lat"), lax.axis_index("lon")
    band, lanes = depth_hbm.shape
    groups = rank // T
    slot = lanes // groups
    half_slot = slot // 2
    edge = 2 * STEPS
    per = 3 * band
    chunk = T * per
    lane8 = lax.broadcasted_iota(jnp.int32, (T, lanes), 1)
    sub8 = lax.broadcasted_iota(jnp.int32, (T, lanes), 0)

    def at(dlat, dlon):
        return (lax.rem(lat + dlat + n_lat, n_lat), lax.rem(lon + dlon + n_lon, n_lon))

    diagonals = [(a, b) for a in (-1, 1) for b in (-1, 1)]
    peers = [(0, b) for b in range(n_lon - 1, 0, -1)] + diagonals + [(a, 0) for a in range(1, n_lat)]
    barrier = pltpu.get_barrier_semaphore()
    for a, b in peers:
        pl.semaphore_signal(barrier, inc=1, device_id=at(a, b), device_id_type=MESH)

    has_up, has_dn = lat > 0, lat < n_lat - 1
    fetched = [
        pltpu.make_async_copy(src, dst, s_in.at[i])
        for i, (src, dst) in enumerate((
            (mean_hbm, aux.at[pl.ds(0, 3 * band)]),
            (depth_hbm, aux.at[pl.ds(3 * band, band)]),
            (fac_hbm, fac_ref),
            (cells_hbm, cells_ref),
            (count_hbm, count_ref),
            (vals_hbm, vals_ref),
            (err_hbm, err_ref),
        ))
    ]
    for copy in fetched:
        copy.start()

    @pl.when(jnp.logical_not(has_up))
    def _():
        up_buf[...] = jnp.zeros_like(up_buf)
        aux_up[...] = jnp.zeros_like(aux_up)
        from_left[0] = jnp.zeros_like(from_left[0])
        from_right[0] = jnp.zeros_like(from_right[0])

    @pl.when(jnp.logical_not(has_dn))
    def _():
        dn_buf[...] = jnp.zeros_like(dn_buf)
        aux_dn[...] = jnp.zeros_like(aux_dn)
        from_left[2] = jnp.zeros_like(from_left[2])
        from_right[2] = jnp.zeros_like(from_right[2])

    def remote(src, dst, ssem, rsem, where):
        return pltpu.make_async_remote_copy(
            src_ref=src, dst_ref=dst, send_sem=ssem, recv_sem=rsem, device_id=where, device_id_type=MESH
        )

    def main_copy(side, g):
        rows = pl.ds(g * chunk, chunk)
        dst = (up_buf, dn_buf)[side]
        return remote(fac_hbm.at[rows], dst.at[rows], s_main.at[side, g], r_main.at[side, g], at(1 - 2 * side, 0))

    def aux_copy(side):
        dst = (aux_up, aux_dn)[side]
        return remote(aux, dst, s_aux.at[side], r_aux.at[side], at(1 - 2 * side, 0))

    def edge_copy(to_right, block):
        dlat = 1 - block
        if to_right:
            return remote(edge_right, from_left.at[block], s_er.at[block], r_er.at[block], at(dlat, 1))
        return remote(edge_left, from_right.at[block], s_el.at[block], r_el.at[block], at(dlat, -1))

    sends = (has_dn, has_up)
    receives = (has_up, has_dn)

    pl.semaphore_wait(barrier, len(peers))
    fetched[0].wait()
    fetched[1].wait()
    for side in range(2):
        @pl.when(sends[side])
        def _(side=side):
            aux_copy(side).start()
            for g in range(groups):
                main_copy(side, g).start()

    def load(ref, f, g):
        return jnp.concatenate([ref[pl.ds(g * chunk + f * band + r, T, stride=per), :] for r in range(band)], 0)

    stack_lane = lax.broadcasted_iota(jnp.int32, (T * band, lanes), 1)
    stack_sub = lax.broadcasted_iota(jnp.int32, (T * band, lanes), 0)

    def seam_tiles(ref, f):
        tiles = roll(load(ref, f, groups - 1), slot * (groups - 1) + half_slot)
        for g in range(groups - 1):
            tiles = jnp.where(
                (stack_lane >= slot * g) & (stack_lane < slot * (g + 1)),
                roll(load(ref, f, g), slot * g + half_slot),
                tiles,
            )
        return tiles

    fetched[2].wait()
    fold = slot // edge
    own_seams = []
    tiles_per = band // fold
    in_slot = lax.rem(lane8, slot)
    for f in range(3):
        seams = seam_tiles(fac_ref, f)
        own_seams.append(seams)
        for t in range(tiles_per):
            right = left = None
            for q in range(fold):
                tile = seams[T * (t * fold + q) : T * (t * fold + q + 1)]
                to_right = roll(tile, edge * q - (half_slot - edge))
                to_left = roll(tile, edge * q - half_slot)
                keep = (in_slot >= edge * q) & (in_slot < edge * (q + 1))
                right = to_right if q == 0 else jnp.where(keep, to_right, right)
                left = to_left if q == 0 else jnp.where(keep, to_left, left)
            row = T * (f * tiles_per + t)
            edge_right[row : row + T, :] = right
            edge_left[row : row + T, :] = left
    aux_edge = None
    for f in range(4):
        tile = roll(aux[f * band : (f + 1) * band, :], 2 * edge * f + edge)
        aux_edge = tile if f == 0 else jnp.where(lane8 >= 2 * edge * f, tile, aux_edge)
    edge_rows = T * 3 * tiles_per
    edge_right[edge_rows:, :] = aux_edge
    edge_left[edge_rows:, :] = aux_edge

    for block in (1, 0, 2):
        def go(block=block):
            edge_copy(True, block).start()
            edge_copy(False, block).start()
        if block == 1:
            go()
        else:
            pl.when(sends[0] if block == 0 else sends[1])(go)

    for copy in fetched[3:]:
        copy.wait()
    cells = cells_ref[...]
    slots = cells.shape[1]
    live = lax.broadcasted_iota(jnp.int32, (1, slots), 1) < count_ref[...]
    weight = jnp.where(live, 1.0, 0.0) / err_ref[...]
    square = weight * weight
    obs_row = jnp.zeros_like(cells)
    for r in range(1, band):
        obs_row = obs_row + jnp.where(cells >= r * lanes, 1, 0)
    obs_col = cells - lanes * obs_row
    row_hot = lax.broadcasted_iota(jnp.int32, (band, slots), 0) == obs_row
    sums = jnp.concatenate(
        [jnp.where(row_hot, square, 0.0), jnp.where(row_hot, square * vals_ref[...], 0.0)], 0
    )
    col_hot = jnp.where(lax.broadcasted_iota(jnp.int32, (lanes, slots), 0) == obs_col, 1.0, 0.0)
    sums = lax.dot_general(
        jnp.concatenate(split(sums, 3), 0), col_hot.astype(jnp.bfloat16), NT, preferred_element_type=jnp.float32
    )
    sums = (sums[4 * band :] + sums[2 * band : 4 * band]) + sums[: 2 * band]
    cell_weight, cell_value = sums[:band], sums[band:]

    half = 0.5 * TIME_STEP
    up_gain = jnp.where(has_up, half, 0.0).astype(jnp.float32)
    down_gain = jnp.where(has_dn, half, 0.0).astype(jnp.float32)

    def spread(tile):
        return jnp.concatenate([jnp.broadcast_to(tile[r : r + 1], (T, lanes)) for r in range(band)], 0)

    for side in range(2):
        @pl.when(receives[side])
        def _(side=side):
            aux_copy(side).wait_recv()
    aux_blocks = (aux_up, aux, aux_dn)
    coef = jnp.concatenate([half * spread(b[3 * band :, :]) for b in aux_blocks], 0)

    blocks = (up_buf, fac_ref, dn_buf)
    for g in range(groups):
        for side in range(2):
            @pl.when(receives[side])
            def _(side=side, g=g):
                main_copy(side, g).wait_recv()
        state = [jnp.concatenate([load(b, f, g) for b in blocks], 0) for f in range(3)]
        state = evolve(*state, coef, up_gain, down_gain, band)
        for f in range(3):
            for r in range(band):
                fc[f * band + r, T * g : T * (g + 1), :] = state[f][T * r : T * (r + 1)]

    edge_copy(True, 1).wait_recv()
    edge_copy(False, 1).wait_recv()
    for side in range(2):
        @pl.when(receives[side])
        def _(side=side):
            edge_copy(True, 2 * side).wait_recv()
            edge_copy(False, 2 * side).wait_recv()

    def aux_pair(b, f):
        own = aux_blocks[b][f * band : (f + 1) * band, :]
        left = from_left[b, edge_rows:, :]
        right = from_right[b, edge_rows:, :]
        strips = jnp.where(lane8 < half_slot, roll(left, half_slot - edge - 2 * edge * f), roll(own, half_slot))
        strips = jnp.where(
            lane8 < slot,
            strips,
            jnp.where(lane8 < slot + half_slot, roll(own, slot + half_slot), roll(right, slot + half_slot - edge - 2 * edge * f)),
        )
        return own, strips

    def mean_group(b, f):
        own, strips = aux_pair(b, f)
        return jnp.concatenate([jnp.where(sub8 == 0, own[r : r + 1], strips[r : r + 1]) for r in range(band)], 0)

    mean_state = [jnp.concatenate([mean_group(b, f) for b in range(3)], 0) for f in range(4)]
    mean_state = evolve(*mean_state[:3], half * mean_state[3], up_gain, down_gain, band)
    mean = []
    for f in range(3):
        strips = roll(mean_state[f], -1, 0)
        low = roll(strips, -half_slot)
        high = roll(strips, lanes - half_slot - slot)
        mean.append(jnp.where(stack_lane < edge, low, jnp.where(stack_lane >= lanes - edge, high, mean_state[f])))

    def repeat_slots(tile):
        tile = jnp.where(lane8 < slot, tile, 0.0)
        total = tile
        for g in range(1, groups):
            total = total + roll(tile, slot * g)
        return total

    strips_of = [aux_pair(b, 3)[1] for b in range(3)]
    coef_left = jnp.concatenate([half * spread(repeat_slots(s)) for s in strips_of], 0)
    coef_right = jnp.concatenate([half * spread(repeat_slots(roll(s, -slot))) for s in strips_of], 0)

    def unpack(ref, b, f, first):
        out = []
        for r in range(band):
            row = T * (f * tiles_per + r // fold)
            out.append(roll(ref[b, row : row + T, :], first - edge * (r % fold)))
        return jnp.concatenate(out, 0)

    low_half = lax.rem(stack_lane, slot) < half_slot
    left_state, right_state = [], []
    for f in range(3):
        lefts, rights = [], []
        for b in range(3):
            seams = own_seams[f] if b == 1 else seam_tiles(blocks[b], f)
            lefts.append(jnp.where(low_half, unpack(from_left, b, f, half_slot - edge), seams))
            rights.append(jnp.where(low_half, seams, unpack(from_right, b, f, half_slot)))
        left_state.append(jnp.concatenate(lefts, 0))
        right_state.append(jnp.concatenate(rights, 0))
    left_state = evolve(*left_state, coef_left, up_gain, down_gain, band)
    right_state = evolve(*right_state, coef_right, up_gain, down_gain, band)
    at_edge = (lane8 < edge) | (lane8 >= lanes - edge)
    for f in range(3):
        seams = jnp.where(low_half, right_state[f], left_state[f])
        for g in range(groups):
            back = roll(seams, -(slot * g + half_slot))
            for r in range(band):
                spot = (f * band + r, slice(T * g, T * (g + 1)), slice(None))
                fc[spot] = jnp.where(at_edge, back[T * r : T * (r + 1)], fc[spot])

    for f in range(3):
        for r in range(band):
            mean_out[f * band + r : f * band + r + 1, :] = mean[f][T * r : T * r + 1]

    lhs, rhs = [], []
    for r in range(band):
        height = fc[r]
        w = cell_weight[r : r + 1]
        drive = cell_value[r : r + 1] - w * mean[0][T * r : T * r + 1]
        lhs.append(height)
        pad = jnp.zeros((lanes // 2 - rank - T, lanes), jnp.float32)
        rhs.append(jnp.concatenate([height * w, jnp.where(sub8 == 0, drive, 0.0), pad], 0))
    gram = lax.dot_general(
        jnp.concatenate(split(jnp.concatenate(lhs, 1), 2), 0),
        jnp.concatenate(split(jnp.concatenate(rhs, 1), 2), 0),
        NT, preferred_element_type=jnp.float32,
    )
    gram = gram[:rank] + gram[rank:]
    gram = gram + roll(gram, lanes // 2)
    hr = rank // 2
    wide = lax.broadcasted_iota(jnp.int32, (hr, lanes), 1)
    mine = jnp.where(wide < lanes // 2, gram[:hr], gram[hr:])

    p1[...] = mine
    def lat_copy(o):
        return remote(p1, ar1.at[o - 1], s1.at[o - 1], r1.at[o - 1], at(o, 0))
    def lon_copy(o):
        return remote(p2, ar2.at[o - 1], s2.at[o - 1], r2.at[o - 1], at(0, o))
    for o in range(1, n_lat):
        lat_copy(o).start()
    for o in range(1, n_lat):
        lat_copy(o).wait_recv()
        mine = mine + ar1[o - 1]
    p2[...] = mine
    for o in range(1, n_lon):
        lon_copy(o).start()
    for o in range(1, n_lon):
        lon_copy(o).wait_recv()
        mine = mine + ar2[o - 1]

    gram_out[...] = mine

    for side in range(2):
        @pl.when(sends[side])
        def _(side=side):
            aux_copy(side).wait_send()
            for g in range(groups):
                main_copy(side, g).wait_send()
            edge_copy(True, 2 * side).wait_send()
            edge_copy(False, 2 * side).wait_send()
    edge_copy(True, 1).wait_send()
    edge_copy(False, 1).wait_send()
    for o in range(1, n_lat):
        lat_copy(o).wait_send()
    for o in range(1, n_lon):
        lon_copy(o).wait_send()


def transform(rank, fc, mean_ref, gram_ref, upd_hbm, out_hbm, upd, res, s_out):
    mine = gram_ref[...]
    lanes = mine.shape[1]
    band = fc.shape[0] // 3
    groups = rank // T
    sub8 = lax.broadcasted_iota(jnp.int32, (T, lanes), 0)
    both = jnp.concatenate([mine, roll(mine, lanes // 2)], 0)
    ri = lax.broadcasted_iota(jnp.int32, (rank, lanes), 0)
    li = lax.broadcasted_iota(jnp.int32, (rank, lanes), 1)
    eyes = jnp.where((li == ri) | (li == ri + lanes // 2), 1.0, 0.0)
    x = jnp.where(li < lanes // 2, both, 0.0) + eyes
    tiles = [x[T * i : T * (i + 1)] for i in range(groups)]
    for b in range(groups):
        cols = {
            (i, q): jnp.broadcast_to(tiles[i][:, T * b + q : T * b + q + 1], (T, lanes))
            for i in range(b, groups)
            for q in range(T)
        }
        for q in range(T):
            inv = 1.0 / cols[b, q][q : q + 1]
            row = tiles[b][q : q + 1]
            heads = [cols[b, p][q : q + 1] for p in range(q + 1, T)]
            for i in range(b, groups):
                if i == b and q == T - 1:
                    continue
                m = cols[i, q] * inv
                if i == b:
                    m = jnp.where(sub8 > q, m, 0.0)
                for p in range(q + 1, T):
                    cols[i, p] = cols[i, p] - m * heads[p - q - 1]
                tiles[i] = tiles[i] - m * row
    x = jnp.concatenate(tiles, 0)
    pivot = jnp.sum(jnp.where(li == ri, x, 0.0), 1, keepdims=True)
    x = x / jnp.sqrt(pivot)
    inverse = jnp.where(li < rank, roll(x, -(lanes // 2)), 0.0)
    z = x[:, rank : rank + 1]
    shift = jnp.sum(inverse * z, 0, keepdims=True)
    coefs = jnp.concatenate([inverse, jnp.where(sub8 == 0, shift, 0.0)], 0)
    high, low = (c.astype(jnp.float32) for c in split(coefs, 2))
    stacked = (high + roll(high, rank) + roll(low, 2 * rank))[:, : 3 * rank].astype(jnp.bfloat16)

    per = 3 * band
    for f in range(3):
        slab = jnp.concatenate([fc[f * band + r] for r in range(band)], 1)
        high, low = split(slab, 2)
        part = jnp.dot(stacked, jnp.concatenate([high, low, high], 0), preferred_element_type=jnp.float32)
        for r in range(band):
            col = part[:, lanes * r : lanes * (r + 1)]
            i = f * band + r
            for g in range(groups):
                res[pl.ds(g * T * per + i, T, stride=per), :] = col[T * g : T * (g + 1)]
            upd[i : i + 1, :] = mean_ref[i : i + 1, :] + col[rank : rank + 1]
    copies = [
        pltpu.make_async_copy(res, out_hbm, s_out.at[0]),
        pltpu.make_async_copy(upd, upd_hbm, s_out.at[1]),
    ]
    for copy in copies:
        copy.start()
    for copy in copies:
        copy.wait()


def in_hbm(x):
    return pltpu.with_memory_space_constraint(x, pltpu.HBM)


def per_device(n_lat, n_lon, background, factor, depth, cells, count, values, error):
    rank, fields, band, lanes = factor.shape
    groups = rank // T
    rows = rank * fields * band
    slots = cells.shape[0]
    assert band == T and 2 * STEPS <= band and rank % T == 0 and fields == 3
    edge_rows = T * (fields * band * groups * 2 * STEPS // lanes + 1)
    vmem = pl.BlockSpec(memory_space=pltpu.VMEM)
    f32 = functools.partial(pltpu.VMEM, dtype=jnp.float32)
    dma = pltpu.SemaphoreType.DMA
    anywhere = pl.BlockSpec(memory_space=pl.ANY)
    forecast, mean, gram = pl.pallas_call(
        functools.partial(kernel, n_lat, n_lon, rank),
        out_shape=(
            jax.ShapeDtypeStruct((fields * band, rank, lanes), jnp.float32),
            jax.ShapeDtypeStruct((fields * band, lanes), jnp.float32),
            jax.ShapeDtypeStruct((rank // 2, lanes), jnp.float32),
        ),
        in_specs=[pl.BlockSpec(memory_space=pltpu.HBM)] * 7,
        out_specs=(vmem, vmem, vmem),
        scratch_shapes=[
            f32((rows, lanes)), pltpu.VMEM((1, slots), jnp.int32), pltpu.VMEM((1, 1), jnp.int32),
            f32((1, slots)), f32((1, slots)), dma((7,)),
            f32((rows, lanes)), f32((rows, lanes)),
            f32((4 * band, lanes)), f32((4 * band, lanes)), f32((4 * band, lanes)),
            f32((edge_rows, lanes)), f32((edge_rows, lanes)),
            f32((3, edge_rows, lanes)), f32((3, edge_rows, lanes)),
            f32((rank // 2, lanes)), f32((rank // 2, lanes)),
            f32((n_lat - 1, rank // 2, lanes)), f32((n_lon - 1, rank // 2, lanes)),
            dma((2, groups)), dma((2, groups)), dma((2,)), dma((2,)),
            dma((3,)), dma((3,)), dma((3,)), dma((3,)),
            dma((n_lat - 1,)), dma((n_lat - 1,)), dma((n_lon - 1,)), dma((n_lon - 1,)),
        ],
        compiler_params=pltpu.CompilerParams(
            collective_id=0, has_side_effects=True, vmem_limit_bytes=32 * 1024 * 1024
        ),
    )(
        in_hbm(background.reshape(fields * band, lanes)), in_hbm(factor.reshape(rows, lanes)), in_hbm(depth),
        in_hbm(cells.reshape(1, slots)), count.reshape(1, 1), in_hbm(values.reshape(1, slots)), in_hbm(error.reshape(1, slots)),
    )
    updated, analysis = pl.pallas_call(
        functools.partial(transform, rank),
        out_shape=(
            jax.ShapeDtypeStruct((fields * band, lanes), jnp.float32),
            jax.ShapeDtypeStruct((rows, lanes), jnp.float32),
        ),
        in_specs=[vmem] * 3,
        out_specs=(anywhere, anywhere),
        scratch_shapes=[f32((fields * band, lanes)), f32((rows, lanes)), dma((2,))],
        compiler_params=pltpu.CompilerParams(vmem_limit_bytes=16 * 1024 * 1024),
    )(forecast, mean, gram)
    return updated.reshape(background.shape), analysis.reshape(factor.shape)


def solution(mesh):
    return jax.shard_map(
        functools.partial(per_device, mesh.shape["lat"], mesh.shape["lon"]),
        mesh=mesh,
        in_specs=(
            P(None, "lat", "lon"),
            P(None, None, "lat", "lon"),
            P("lat", "lon"),
            P(("lat", "lon")),
            P(("lat", "lon")),
            P(("lat", "lon")),
            P(("lat", "lon")),
        ),
        out_specs=(P(None, "lat", "lon"), P(None, None, "lat", "lon")),
        check_vma=False,
    )
```
